32 devices in a mesh: strip: 8 (over y, x, core), lag: 4 (over z).
Axes of the slice: x: 2, y: 2, z: 4, core: 2. Of those that a mesh axis runs over, the one named last changes fastest.
Arguments:
- image_grad: float32 [128, 512, 1024], P('lag', 'strip'), may hold values from -0.4 to 0.4
- source_field: float32 [2, 512, 1024], P(None, None, 'strip'), may hold values from -6 to 6
- receiver_field: float32 [2, 512, 1024], P(None, None, 'strip'), may hold values from -6 to 6
Outputs:
- source_adjoint: float32 [2, 512, 1024], P(None, 'strip', 'lag')
- receiver_adjoint: float32 [2, 512, 1024], P(None, 'strip', 'lag')
The draws below stay inside these ranges and needn't reach their ends.
All inputs are finite; a program needn't handle non-finite values.
Results may differ from the reference program's by a relative error of at most 0.0003.
Values sent between devices are 32-bit elements; how exact they have to be, the bound alone decides.
No kernel may reach another device: no remote copies, remote signals or barrier semaphores. Data moves between devices by JAX's collectives and lax.ppermute only.
A program may use at most 128 MiB of HBM per device.

```python
import jax
import jax.numpy as jnp
from jax import lax

NX = 1024
NH = 128
SNAP = 2
NZ = 512


def level_of(rng, extent, shards, low, high):
    def one(axis_at, shards_of):
        steps = jax.random.uniform(jax.random.fold_in(jax.random.fold_in(rng, 6), axis_at), (shards_of,), jnp.float32, low / len(shards), high / len(shards))
        return jnp.repeat(jnp.exp(steps), extent[axis_at] // shards_of).reshape((-1,) + (1,) * (len(extent) - axis_at - 1))

    loudness = one(*shards[0])
    for cut in shards[1:]:
        loudness = loudness * one(*cut)
    return loudness


def bell_draw(rng, shape, scale, bound, split=(), kind=jnp.bfloat16):
    level = level_of(rng, shape, split, -0.22, 0.18) if split else 1.0
    drawn = jax.random.normal(rng, shape, jnp.float32) * scale * level
    return jnp.minimum(jnp.maximum(drawn, -bound), bound).astype(kind)


def setup_inputs(seed: int = 0) -> dict:
    key_list = jax.random.split(jax.random.key(seed), 4)
    image_grad = bell_draw(key_list[0], (NH, NZ, NX), 0.05, 0.4, ((0, 4), (1, 8)), jnp.float32)
    source_field = bell_draw(key_list[1], (SNAP, NZ, NX), 1.0, 6.0, ((2, 8),), jnp.float32)
    receiver_field = bell_draw(key_list[2], (SNAP, NZ, NX), 1.0, 6.0, ((2, 8),), jnp.float32)
    return dict(image_grad=image_grad, source_field=source_field, receiver_field=receiver_field)


def pad_cells(values, width_cells):
    return jnp.pad(values, [(0, 0)] * (values.ndim - 1) + [(width_cells, width_cells)])


def shift_cells(padded_values, offset, width_cells):
    start = (width_cells + offset).astype(jnp.int32)
    return lax.dynamic_slice_in_dim(padded_values, start, width_cells, padded_values.ndim - 1)


def laplace_filter(slab_now):
    padded = jnp.pad(slab_now, 1)
    center = padded[1:-1, 1:-1]
    return 2.0 * center - 0.25 * (padded[2:, 1:-1] + padded[:-2, 1:-1] + padded[1:-1, 2:] + padded[1:-1, :-2])


def reference(image_grad, source_field, receiver_field):
    width_cells = image_grad.shape[2]
    source = pad_cells(source_field, width_cells)
    receiver = pad_cells(receiver_field, width_cells)
    empty_sum = jnp.zeros((source_field.shape[0], image_grad.shape[1], width_cells), jnp.float32)

    def lag_step(totals, lag_number):
        source_total, receiver_total = totals
        slab_now = laplace_filter(lax.dynamic_index_in_dim(image_grad, lag_number, 0, keepdims=False))
        slab_pad = pad_cells(slab_now, width_cells)
        offset = lag_number - NH // 2
        source_total = source_total + shift_cells(slab_pad, offset, width_cells)[None] * shift_cells(receiver, 2 * offset, width_cells)
        receiver_total = receiver_total + shift_cells(slab_pad, -offset, width_cells)[None] * shift_cells(source, -2 * offset, width_cells)
        return (source_total, receiver_total), None

    (source_adjoint, receiver_adjoint), unused = lax.scan(lag_step, (empty_sum, empty_sum), jnp.arange(NH, dtype=jnp.int32))
    return source_adjoint, receiver_adjoint
```

```python
import functools

import jax
import jax.numpy as jnp
from jax import lax
from jax.experimental import pallas as pl
from jax.experimental.pallas import tpu as pltpu
from jax.sharding import PartitionSpec as P

LANES = 128
ROWS = 8
CLASSES = 4
VMEM_BYTES = 56 * 1024 * 1024


def chain_halo(rows, axis, step):
    count = lax.axis_size(axis)
    pairs = [(i, i + step) for i in range(count) if 0 <= i + step < count]
    return lax.ppermute(rows, axis, pairs)


def filter_kernel(grad_hbm, above_ref, below_ref, src_ref, rec_ref):
    lag_count, depth, width = grad_hbm.shape
    tiles = width // LANES
    groups = depth // ROWS

    def body(grad_ref, top_ref, low_ref):
        group_at = pl.program_id(0)
        row = lax.broadcasted_iota(jnp.int32, (ROWS, LANES), 0)
        lane = lax.broadcasted_iota(jnp.int32, (ROWS, LANES), 1)
        zero = jnp.zeros((ROWS, LANES), jnp.float32)

        def tile_of(within, group, tile):
            return grad_ref[within, pl.ds(group * ROWS, ROWS), pl.ds(tile * LANES, LANES)]

        for within in range(CLASSES):
            lag = group_at * CLASSES + within
            src_move = lag_count - CLASSES * group_at + within
            rec_move = CLASSES + CLASSES * group_at - within
            for group in range(groups):
                center = [tile_of(within, group, t) for t in range(tiles)]
                left = [pltpu.roll(v, 1, 1) for v in center]
                right = [pltpu.roll(v, LANES - 1, 1) for v in center]
                src_before, rec_before = zero, zero
                for t in range(tiles):
                    mid = center[t]
                    if group:
                        before = tile_of(within, group - 1, t)
                        above = jnp.where(row == 0, pltpu.roll(before, 1, 0), pltpu.roll(mid, 1, 0))
                    else:
                        edge = top_ref[pl.ds(within, 1), pl.ds(t * LANES, LANES)]
                        above = jnp.where(row == 0, edge, pltpu.roll(mid, 1, 0))
                    if group + 1 < groups:
                        after = tile_of(within, group + 1, t)
                        below = jnp.where(
                            row == ROWS - 1, pltpu.roll(after, ROWS - 1, 0), pltpu.roll(mid, ROWS - 1, 0)
                        )
                    else:
                        edge = low_ref[pl.ds(within, 1), pl.ds(t * LANES, LANES)]
                        below = jnp.where(row == ROWS - 1, edge, pltpu.roll(mid, ROWS - 1, 0))
                    west = jnp.where(lane == 0, left[t - 1] if t else zero, left[t])
                    east = jnp.where(
                        lane == LANES - 1, right[t + 1] if t + 1 < tiles else zero, right[t]
                    )
                    value = 2.0 * mid - 0.25 * ((above + below) + (west + east))
                    src_turned = pltpu.roll(value, src_move, 1)
                    rec_turned = pltpu.roll(value, rec_move, 1)
                    rows = pl.ds(group * ROWS, ROWS)
                    src_ref[lag, t, rows] = jnp.where(lane < src_move, src_before, src_turned)
                    rec_ref[lag, t, rows] = jnp.where(lane < rec_move, rec_before, rec_turned)
                    src_before, rec_before = src_turned, rec_turned
                rows = pl.ds(group * ROWS, ROWS)
                src_ref[lag, tiles, rows] = jnp.where(lane < src_move, src_before, 0.0)
                rec_ref[lag, tiles, rows] = jnp.where(lane < rec_move, rec_before, 0.0)

    pltpu.emit_pipeline(
        body,
        grid=(lag_count // CLASSES,),
        in_specs=[
            pl.BlockSpec((CLASSES, depth, width), lambda i: (i, 0, 0)),
            pl.BlockSpec((None, CLASSES, width), lambda i: (i, 0, 0)),
            pl.BlockSpec((None, CLASSES, width), lambda i: (i, 0, 0)),
        ],
        out_specs=[],
    )(grad_hbm, above_ref, below_ref)


def filter_both(image_grad, above, below):
    lag_count, depth, width = image_grad.shape
    shape = (lag_count, width // LANES + 1, depth, LANES)
    return pl.pallas_call(
        filter_kernel,
        out_shape=[jax.ShapeDtypeStruct(shape, jnp.float32)] * 2,
        in_specs=[pl.BlockSpec(memory_space=pl.ANY)] * 3,
        out_specs=[pl.BlockSpec(memory_space=pltpu.VMEM)] * 2,
        compiler_params=pltpu.CompilerParams(vmem_limit_bytes=VMEM_BYTES),
        name="filter_both",
    )(image_grad, above, below)


def sum_kernel(sign, moved_ref, field_ref, keep_ref, send_ref, padded, turned, sums):
    lag_count, wide, depth, _ = moved_ref.shape
    snaps, tiles = field_ref.shape[0], field_ref.shape[1]
    groups = depth // ROWS
    steps = lag_count // CLASSES
    place = lax.axis_index("lag")
    places = lax.axis_size("lag")
    first = place * lag_count - places * lag_count // 2
    lane = lax.broadcasted_iota(jnp.int32, (depth, LANES), 1)
    blank = jnp.zeros((depth, LANES), jnp.float32)

    for snap in range(snaps):
        padded[snap, 0] = blank
        for t in range(tiles):
            padded[snap, t + 1] = field_ref[snap, t]
        for t in range(tiles + 1, tiles + 3):
            padded[snap, t] = blank

    def turn(step, carry):
        if sign > 0:
            move = lag_count - first - 2 * CLASSES * step
        else:
            move = CLASSES + first + 2 * CLASSES * step
        back = jnp.where(move < 0, 1, 0)
        move = move + LANES * back
        for snap in range(snaps):
            before = pltpu.roll(padded[snap, back], move, 1)
            for t in range(wide):
                after = pltpu.roll(padded[snap, t + back + 1], move, 1)
                turned[step, snap, t] = jnp.where(lane < move, before, after)
                before = after
        return carry

    lax.fori_loop(0, steps, turn, 0)

    for cls in range(CLASSES):
        for snap in range(snaps):
            sums[cls, snap, 0] = blank

    def block(at, carry):
        t = at // groups
        rows = pl.ds((at % groups) * ROWS, ROWS)
        totals = [[None] * snaps for _ in range(CLASSES)]
        for step in range(steps):
            fields = [turned[step, snap, t, rows] for snap in range(snaps)]
            for cls in range(CLASSES):
                slab = moved_ref[step * CLASSES + cls, t, rows]
                for snap in range(snaps):
                    term = slab * fields[snap]
                    totals[cls][snap] = term if step == 0 else totals[cls][snap] + term
        for cls in range(CLASSES):
            for snap in range(snaps):
                sums[cls, snap, t + 1, rows] = totals[cls][snap]
        return carry

    lax.fori_loop(0, wide * groups, block, 0)

    halves = tiles // places

    def finish(target, slot, source):
        for half in range(halves):
            t = source * halves + half
            for snap in range(snaps):
                total = None
                for cls in range(CLASSES):
                    if sign > 0:
                        move = first + lag_count + 2 * cls
                    else:
                        move = CLASSES - first - 2 * cls
                    back = jnp.where(move < 0, 1, 0)
                    move = LANES - (move + LANES * back)
                    low = pltpu.roll(sums[cls, snap, t + 1 - back], move, 1)
                    high = pltpu.roll(sums[cls, snap, t + 2 - back], move, 1)
                    term = jnp.where(lane < move, low, high)
                    total = term if total is None else total + term
                target[slot, snap, :, pl.ds(half * LANES, LANES)] = total

    other = place + 1 - 2 * lax.rem(place, 2)
    finish(send_ref, 0, other)
    finish(send_ref, 1, places - 1 - other)
    finish(keep_ref, 0, place)
    finish(keep_ref, 1, places - 1 - place)


def sum_lags(sign, moved, field):
    lag_count, wide, depth, _ = moved.shape
    snaps, tiles = field.shape[0], field.shape[1]
    places = lax.axis_size("lag")
    part = jax.ShapeDtypeStruct((2, snaps, depth, tiles * LANES // places), jnp.float32)
    return pl.pallas_call(
        functools.partial(sum_kernel, sign),
        out_shape=[part, part],
        in_specs=[pl.BlockSpec(memory_space=pltpu.VMEM)] * 2,
        out_specs=[pl.BlockSpec(memory_space=pltpu.VMEM)] * 2,
        scratch_shapes=[
            pltpu.VMEM((snaps, tiles + 3, depth, LANES), jnp.float32),
            pltpu.VMEM((lag_count // CLASSES, snaps, wide, depth, LANES), jnp.float32),
            pltpu.VMEM((CLASSES, snaps, wide + 1, depth, LANES), jnp.float32),
        ],
        compiler_params=pltpu.CompilerParams(vmem_limit_bytes=VMEM_BYTES),
        name="sum_lags",
    )(moved, field)


def rows_of_field(field):
    count = lax.axis_size("strip")
    snaps, all_rows, columns = field.shape
    depth = all_rows // count
    cut = field.reshape(snaps, count, depth, columns)
    cut = lax.all_to_all(cut, "strip", split_axis=1, concat_axis=1, tiled=True)
    if columns == LANES:
        return cut
    whole = cut.transpose(0, 2, 1, 3).reshape(snaps, depth, count * columns // LANES, LANES)
    return whole.transpose(0, 2, 1, 3)


def exchange(parts, distance):
    count = lax.axis_size("lag")
    return lax.ppermute(parts, "lag", [(i, i ^ distance) for i in range(count)])


def sum_places(keep, send):
    both = keep + exchange(send, 1)
    return both[0] + exchange(both[1], 3)


def local(image_grad, source_field, receiver_field):
    lag_count, depth, width = image_grad.shape
    receiver = rows_of_field(receiver_field)
    source = rows_of_field(source_field)
    steps = (lag_count // CLASSES, CLASSES, width)
    above = chain_halo(image_grad[:, depth - 1], "strip", 1).reshape(steps)
    below = chain_halo(image_grad[:, 0], "strip", -1).reshape(steps)
    for_source, for_receiver = filter_both(image_grad, above, below)
    keep, send = sum_lags(1, for_source, receiver)
    source_adjoint = sum_places(keep, send)
    keep, send = sum_lags(-1, for_receiver, source)
    receiver_adjoint = sum_places(keep, send)
    return source_adjoint, receiver_adjoint


def solution(mesh):
    in_specs = (P("lag", "strip", None), P(None, None, "strip"), P(None, None, "strip"))
    out_specs = (P(None, "strip", "lag"), P(None, "strip", "lag"))
    return jax.shard_map(local, mesh=mesh, in_specs=in_specs, out_specs=out_specs, check_vma=False)
```

```python
import functools

import jax
import jax.numpy as jnp
from jax import lax
from jax.experimental import pallas as pl
from jax.experimental.pallas import tpu as pltpu
from jax.sharding import PartitionSpec as P

LANES = 128
ROWS = 8
CLASSES = 4
VMEM_BYTES = 24 * 1024 * 1024

whole_vmem = pl.BlockSpec(memory_space=pltpu.VMEM)
anywhere = pl.BlockSpec(memory_space=pl.ANY)


def chain_halo(rows, axis, step):
    count = lax.axis_size(axis)
    pairs = [(i, i + step) for i in range(count) if 0 <= i + step < count]
    return lax.ppermute(rows, axis, pairs)


def filter_kernel(pad, grad_hbm, above_hbm, below_hbm, out_ref, center_t, upright_t):
    lag_count, depth, width = grad_hbm.shape
    half = lag_count // 2
    tiles = width // LANES
    out_ref[:, pl.ds(0, pad)] = jnp.zeros((half, pad, LANES), jnp.float32)
    out_ref[:, pl.ds(pad + width, pad)] = jnp.zeros((half, pad, LANES), jnp.float32)
    center_t[pl.ds(0, ROWS)] = jnp.zeros((ROWS, LANES), jnp.float32)
    center_t[pl.ds(ROWS + width, ROWS)] = jnp.zeros((ROWS, LANES), jnp.float32)

    def body(low_ref, high_ref, low_above, high_above, low_below, high_below):
        pair = pl.program_id(0)
        row = lax.broadcasted_iota(jnp.int32, (depth, LANES), 0)
        slabs = ((low_ref, low_above, low_below), (high_ref, high_above, high_below))
        for t in range(tiles):
            lanes = pl.ds(t * LANES, LANES)
            mids, uprights = [], []
            for slab, above, below in slabs:
                mid = slab[:, lanes]
                up = jnp.where(row == 0, above[:, lanes], pltpu.roll(mid, 1, 0))
                down = jnp.where(row == depth - 1, below[:, lanes], pltpu.roll(mid, depth - 1, 0))
                mids.append(mid)
                uprights.append(2.0 * mid - 0.25 * (up + down))
            center_t[pl.ds(ROWS + t * LANES, LANES)] = jnp.concatenate(mids, 0).T
            upright_t[pl.ds(t * LANES, LANES)] = jnp.concatenate(uprights, 0).T
        for t in range(tiles):
            rows = pl.ds(t * LANES, LANES)
            west = center_t[pl.ds(ROWS - 1 + t * LANES, LANES)]
            east = center_t[pl.ds(ROWS + 1 + t * LANES, LANES)]
            out_ref[pair, pl.ds(pad + t * LANES, LANES)] = upright_t[rows] - 0.25 * (west + east)

    slab = pl.BlockSpec((None, depth, width), lambda i: (i, 0, 0))
    slab_half = pl.BlockSpec((None, depth, width), lambda i: (i + half, 0, 0))
    edge = pl.BlockSpec((None, 1, width), lambda i: (i, 0, 0))
    edge_half = pl.BlockSpec((None, 1, width), lambda i: (i + half, 0, 0))
    pltpu.emit_pipeline(
        body,
        grid=(half,),
        in_specs=[slab, slab_half, edge, edge_half, edge, edge_half],
        out_specs=[],
    )(grad_hbm, grad_hbm, above_hbm, above_hbm, below_hbm, below_hbm)


def filter_slabs(image_grad, above, below, pad):
    lag_count, depth, width = image_grad.shape
    return pl.pallas_call(
        functools.partial(filter_kernel, pad),
        out_shape=jax.ShapeDtypeStruct((lag_count // 2, width + 2 * pad, 2 * depth), jnp.float32),
        in_specs=[anywhere] * 3,
        out_specs=whole_vmem,
        scratch_shapes=[
            pltpu.VMEM((width + 2 * ROWS, LANES), jnp.float32),
            pltpu.VMEM((width, LANES), jnp.float32),
        ],
        compiler_params=pltpu.CompilerParams(vmem_limit_bytes=VMEM_BYTES),
        cost_estimate=pl.CostEstimate(
            flops=8 * lag_count * depth * width, bytes_accessed=8 * lag_count * depth * width, transcendentals=0
        ),
        name="filter_slabs",
    )(image_grad, above, below)


def sum_kernel(sign, places, slab_ref, field_ref, keep_ref, send_ref, paired, acc):
    half, slab_rows, _ = slab_ref.shape
    width = field_ref.shape[0]
    pad = (slab_rows - width) // 2
    lag_count = 2 * half
    margin = 2 * pad + 2 * half
    place = lax.axis_index("lag")
    first = place * lag_count - pad
    spread = width + half
    block_rows = ROWS * max(m for m in range(1, 11) if spread // ROWS % m == 0)
    low_at = 0 if sign > 0 else half
    high_at = half - low_at

    for snap in range(2):
        blank = jnp.zeros((margin + half, LANES), jnp.float32)
        paired[snap, pl.ds(0, margin)] = blank[:margin]
        paired[snap, pl.ds(margin + width, margin)] = blank[:margin]
    low = lax.broadcasted_iota(jnp.int32, (LANES, LANES), 1) < LANES // 2
    edge = jnp.zeros((half, LANES), jnp.float32)
    field = field_ref[...]
    lower = lax.broadcasted_iota(jnp.int32, (spread, LANES), 1) < LANES // 2
    if sign > 0:
        here = jnp.concatenate([edge, field], 0)
        there = jnp.concatenate([field, edge], 0)
        start = margin - half
    else:
        here = jnp.concatenate([field, edge], 0)
        there = jnp.concatenate([edge, field], 0)
        start = margin
    paired[0, pl.ds(start, spread)] = jnp.where(lower, here, pltpu.roll(there, LANES // 2, 1))
    paired[1, pl.ds(start, spread)] = jnp.where(lower, pltpu.roll(here, LANES // 2, 1), there)

    tall = block_rows // ROWS
    per_class = half // CLASSES

    def block(at, carry):
        y = at * block_rows - low_at
        slab_at = pl.multiple_of(pad + y + sign * first, ROWS)
        field_at = pl.multiple_of(margin + y + sign * 2 * first, ROWS)
        totals = [[None] * tall for _ in range(2)]
        for cls in range(CLASSES):
            held = {}
            for step in range(per_class):
                lag = step * CLASSES + cls
                for up in range(tall):
                    slab = slab_ref[lag, pl.ds(slab_at + sign * lag + up * ROWS, ROWS)]
                    for snap in range(2):
                        row = sign * 2 * lag + up * ROWS
                        if (snap, row) not in held:
                            held[snap, row] = paired[snap, pl.ds(field_at + row, ROWS)]
                        term = slab * held[snap, row]
                        total = totals[snap][up]
                        totals[snap][up] = term if total is None else total + term
        for snap in range(2):
            for up in range(tall):
                rows = pl.multiple_of(at * block_rows + up * ROWS, ROWS)
                acc[snap, pl.ds(rows, ROWS)] = totals[snap][up]
        return carry

    lax.fori_loop(0, spread // block_rows, block, 0)

    part = width // places

    def finish(target, slot, source):
        for piece in range(part // LANES):
            x = pl.multiple_of(source * part + piece * LANES, LANES)
            at_low = pl.ds(x + low_at, LANES)
            at_high = pl.ds(x + high_at, LANES)
            straight = jnp.where(low, acc[0, at_low], acc[1, at_high])
            crossed = jnp.where(low, acc[1, at_low], acc[0, at_high])
            target[slot, pl.ds(piece * LANES, LANES)] = straight + pltpu.roll(crossed, LANES // 2, 1)

    other = place + 1 - 2 * lax.rem(place, 2)
    finish(send_ref, 0, other)
    finish(send_ref, 1, places - 1 - other)
    finish(keep_ref, 0, place)
    finish(keep_ref, 1, places - 1 - place)


def sum_lags(sign, slabs, field):
    half, slab_rows, _ = slabs.shape
    width = field.shape[0]
    pad = (slab_rows - width) // 2
    margin = 2 * pad + 2 * half
    places = lax.axis_size("lag")
    part = jax.ShapeDtypeStruct((2, width // places, LANES), jnp.float32)
    return pl.pallas_call(
        functools.partial(sum_kernel, sign, places),
        out_shape=[part, part],
        in_specs=[whole_vmem] * 2,
        out_specs=[whole_vmem] * 2,
        scratch_shapes=[
            pltpu.VMEM((2, width + 2 * margin, LANES), jnp.float32),
            pltpu.VMEM((2, width + half, LANES), jnp.float32),
        ],
        compiler_params=pltpu.CompilerParams(vmem_limit_bytes=VMEM_BYTES),
        cost_estimate=pl.CostEstimate(
            flops=8 * half * width * LANES, bytes_accessed=4 * half * slab_rows * LANES, transcendentals=0
        ),
        name="sum_lags",
    )(slabs, field)


def turn_kernel(*refs):
    half = len(refs) // 2
    for field_ref, out_ref in zip(refs[:half], refs[half:]):
        snaps = field_ref.shape[0]
        count, columns, lanes = out_ref.shape
        depth = lanes // snaps
        for at in range(count):
            rows = [field_ref[s, pl.ds(at * depth, depth)] for s in range(snaps)]
            out_ref[at] = jnp.concatenate(rows, 0).T


def cut_fields(*fields):
    count = lax.axis_size("strip")
    snaps, all_rows, columns = fields[0].shape
    depth = all_rows // count
    if columns != LANES:
        return [
            f.reshape(snaps, count, depth, columns).transpose(1, 3, 0, 2).reshape(count, columns, snaps * depth)
            for f in fields
        ]
    out = jax.ShapeDtypeStruct((count, columns, snaps * depth), jnp.float32)
    return pl.pallas_call(
        turn_kernel,
        out_shape=[out] * len(fields),
        in_specs=[whole_vmem] * len(fields),
        out_specs=[whole_vmem] * len(fields),
        name="cut_fields",
    )(*fields)


def rows_of_field(cut):
    whole = lax.all_to_all(cut, "strip", split_axis=0, concat_axis=0, tiled=True)
    return whole.reshape(whole.shape[0] * whole.shape[1], whole.shape[2])


def exchange(parts, distance):
    count = lax.axis_size("lag")
    return lax.ppermute(parts, "lag", [(i, i ^ distance) for i in range(count)])


def turn_back_kernel(first_ref, second_ref, out_ref):
    snaps, depth, _ = out_ref.shape
    for at in range(first_ref.shape[0] // LANES):
        rows = pl.ds(at * LANES, LANES)
        turned = (first_ref[rows] + second_ref[rows]).T
        for snap in range(snaps):
            out_ref[snap, :, rows] = turned[snap * depth : (snap + 1) * depth]


def sum_places(keep, send, snaps):
    both = keep + exchange(send, 1)
    rows, lanes = both.shape[1:]
    return pl.pallas_call(
        turn_back_kernel,
        out_shape=jax.ShapeDtypeStruct((snaps, lanes // snaps, rows), jnp.float32),
        in_specs=[whole_vmem] * 2,
        out_specs=whole_vmem,
        name="turn_back",
    )(both[0], exchange(both[1], 3))


def local(image_grad, source_field, receiver_field):
    lag_count, depth, width = image_grad.shape
    snaps = source_field.shape[0]
    pad = lax.axis_size("lag") * lag_count // 2
    receiver_cut, source_cut = cut_fields(receiver_field, source_field)
    receiver = rows_of_field(receiver_cut)
    source = rows_of_field(source_cut)
    above = chain_halo(image_grad[:, depth - 1 :], "strip", 1)
    below = chain_halo(image_grad[:, :1], "strip", -1)
    slabs = filter_slabs(image_grad, above, below, pad)
    source_adjoint = sum_places(*sum_lags(1, slabs, receiver), snaps)
    receiver_adjoint = sum_places(*sum_lags(-1, slabs, source), snaps)
    return source_adjoint, receiver_adjoint


def solution(mesh):
    in_specs = (P("lag", "strip", None), P(None, None, "strip"), P(None, None, "strip"))
    out_specs = (P(None, "strip", "lag"), P(None, "strip", "lag"))
    return jax.shard_map(local, mesh=mesh, in_specs=in_specs, out_specs=out_specs, check_vma=False)
```

```python
import functools

import jax
import jax.numpy as jnp
from jax import lax
from jax.experimental import pallas as pl
from jax.experimental.pallas import tpu as pltpu
from jax.sharding import PartitionSpec as P

LANES = 128
ROWS = 8
CLASSES = 4
PAIRS = 4
FILTER_BYTES = 24 * 1024 * 1024
SUM_BYTES = 8 * 1024 * 1024
SMALL_BYTES = 4 * 1024 * 1024

whole_vmem = pl.BlockSpec(memory_space=pltpu.VMEM)


def chain_halo(rows, axis, step):
    count = lax.axis_size(axis)
    pairs = [(i, i + step) for i in range(count) if 0 <= i + step < count]
    return lax.ppermute(rows, axis, pairs)


def filter_kernel(pad, grad_hbm, above_ref, below_ref, out_ref, *turned):
    lag_count, depth, width = grad_hbm.shape
    half = lag_count // 2
    tiles = width // LANES
    centers, uprights = turned[:PAIRS], turned[PAIRS:]
    out_ref[:, pl.ds(0, pad)] = jnp.zeros((half, pad, LANES), jnp.float32)
    out_ref[:, pl.ds(pad + width, pad)] = jnp.zeros((half, pad, LANES), jnp.float32)
    for center_t in centers:
        center_t[pl.ds(0, ROWS)] = jnp.zeros((ROWS, LANES), jnp.float32)
        center_t[pl.ds(ROWS + width, ROWS)] = jnp.zeros((ROWS, LANES), jnp.float32)

    def body(low_ref, high_ref):
        step = pl.program_id(0)
        row = lax.broadcasted_iota(jnp.int32, (depth, LANES), 0)

        def turn(within, t):
            lanes = pl.ds(t * LANES, LANES)
            mids, stencils = [], []
            for slab, shift in ((low_ref, 0), (high_ref, half)):
                lag = step * PAIRS + within + shift
                mid = slab[within, :, lanes]
                up = jnp.where(row == 0, above_ref[lag, :, lanes], pltpu.roll(mid, 1, 0))
                down = jnp.where(row == depth - 1, below_ref[lag, :, lanes], pltpu.roll(mid, depth - 1, 0))
                mids.append(mid)
                stencils.append(2.0 * mid - 0.25 * (up + down))
            centers[within][pl.ds(ROWS + t * LANES, LANES)] = jnp.concatenate(mids, 0).T
            uprights[within][pl.ds(t * LANES, LANES)] = jnp.concatenate(stencils, 0).T

        def join(within, t):
            west = centers[within][pl.ds(ROWS - 1 + t * LANES, LANES)]
            east = centers[within][pl.ds(ROWS + 1 + t * LANES, LANES)]
            upright = uprights[within][pl.ds(t * LANES, LANES)]
            out_ref[step * PAIRS + within, pl.ds(pad + t * LANES, LANES)] = upright - 0.25 * (west + east)

        for within in range(PAIRS + 1):
            for t in range(tiles):
                if within < PAIRS:
                    turn(within, t)
                if within:
                    join(within - 1, t)

    pltpu.emit_pipeline(
        body,
        grid=(half // PAIRS,),
        in_specs=[
            pl.BlockSpec((PAIRS, depth, width), lambda i: (i, 0, 0)),
            pl.BlockSpec((PAIRS, depth, width), lambda i: (i + half // PAIRS, 0, 0)),
        ],
        out_specs=[],
    )(grad_hbm, grad_hbm)


def filter_slabs(image_grad, above, below, pad):
    lag_count, depth, width = image_grad.shape
    return pl.pallas_call(
        functools.partial(filter_kernel, pad),
        out_shape=jax.ShapeDtypeStruct((lag_count // 2, width + 2 * pad, 2 * depth), jnp.float32),
        in_specs=[pl.BlockSpec(memory_space=pltpu.HBM), whole_vmem, whole_vmem],
        out_specs=whole_vmem,
        scratch_shapes=[pltpu.VMEM((width + 2 * ROWS, LANES), jnp.float32)] * PAIRS
        + [pltpu.VMEM((width, LANES), jnp.float32)] * PAIRS,
        compiler_params=pltpu.CompilerParams(vmem_limit_bytes=FILTER_BYTES),
        cost_estimate=pl.CostEstimate(
            flops=8 * lag_count * depth * width, bytes_accessed=8 * lag_count * depth * width, transcendentals=0
        ),
        name="filter_slabs",
    )(image_grad, above, below)


def sum_kernel(sign, places, where_at, slab_ref, *refs):
    pieces, (keep_ref, send_ref, field_ref, paired, acc) = refs[:-5], refs[-5:]
    half, slab_rows, _ = slab_ref.shape
    width = field_ref.shape[0]
    if where_at is None:
        field_ref[...] = pieces[0][...]
    else:
        columns = pieces[0].shape[-2]
        strip = lax.axis_index("strip")
        for index, block, distance in where_at:
            rows = pl.multiple_of((strip ^ distance) * columns, columns)
            field_ref[pl.ds(rows, columns)] = pieces[index][block]
    pad = (slab_rows - width) // 2
    lag_count = 2 * half
    margin = 2 * pad + 2 * half
    place = lax.axis_index("lag")
    first = place * lag_count - pad
    spread = width + half
    block_rows = ROWS * max(m for m in range(1, 11) if spread // ROWS % m == 0)
    low_at = 0 if sign > 0 else half
    high_at = half - low_at

    for snap in range(2):
        blank = jnp.zeros((margin + half, LANES), jnp.float32)
        paired[snap, pl.ds(0, margin)] = blank[:margin]
        paired[snap, pl.ds(margin + width, margin)] = blank[:margin]
    low = lax.broadcasted_iota(jnp.int32, (LANES, LANES), 1) < LANES // 2
    edge = jnp.zeros((half, LANES), jnp.float32)
    field = field_ref[...]
    lower = lax.broadcasted_iota(jnp.int32, (spread, LANES), 1) < LANES // 2
    if sign > 0:
        here = jnp.concatenate([edge, field], 0)
        there = jnp.concatenate([field, edge], 0)
        start = margin - half
    else:
        here = jnp.concatenate([field, edge], 0)
        there = jnp.concatenate([edge, field], 0)
        start = margin
    paired[0, pl.ds(start, spread)] = jnp.where(lower, here, pltpu.roll(there, LANES // 2, 1))
    paired[1, pl.ds(start, spread)] = jnp.where(lower, pltpu.roll(here, LANES // 2, 1), there)

    tall = block_rows // ROWS
    per_class = half // CLASSES

    def block(at, carry):
        y = at * block_rows - low_at
        slab_at = pl.multiple_of(pad + y + sign * first, ROWS)
        field_at = pl.multiple_of(margin + y + sign * 2 * first, ROWS)
        totals = [[None] * tall for _ in range(2)]
        for cls in range(CLASSES):
            held = {}
            for step in range(per_class):
                lag = step * CLASSES + cls
                for up in range(tall):
                    slab = slab_ref[lag, pl.ds(slab_at + sign * lag + up * ROWS, ROWS)]
                    for snap in range(2):
                        row = sign * 2 * lag + up * ROWS
                        if (snap, row) not in held:
                            held[snap, row] = paired[snap, pl.ds(field_at + row, ROWS)]
                        term = slab * held[snap, row]
                        total = totals[snap][up]
                        totals[snap][up] = term if total is None else total + term
        for snap in range(2):
            for up in range(tall):
                rows = pl.multiple_of(at * block_rows + up * ROWS, ROWS)
                acc[snap, pl.ds(rows, ROWS)] = totals[snap][up]
        return carry

    lax.fori_loop(0, spread // block_rows, block, 0)

    part = width // places

    def finish(target, slot, source):
        for piece in range(part // LANES):
            x = pl.multiple_of(source * part + piece * LANES, LANES)
            at_low = pl.ds(x + low_at, LANES)
            at_high = pl.ds(x + high_at, LANES)
            straight = jnp.where(low, acc[0, at_low], acc[1, at_high])
            crossed = jnp.where(low, acc[1, at_low], acc[0, at_high])
            target[slot, pl.ds(piece * LANES, LANES)] = straight + pltpu.roll(crossed, LANES // 2, 1)

    other = place + 1 - 2 * lax.rem(place, 2)
    finish(send_ref, 0, other)
    finish(send_ref, 1, places - 1 - other)
    finish(keep_ref, 0, place)
    finish(keep_ref, 1, places - 1 - place)


def sum_lags(sign, slabs, pieces, where_at, width):
    half, slab_rows, _ = slabs.shape
    pad = (slab_rows - width) // 2
    margin = 2 * pad + 2 * half
    places = lax.axis_size("lag")
    part = jax.ShapeDtypeStruct((2, width // places, LANES), jnp.float32)
    return pl.pallas_call(
        functools.partial(sum_kernel, sign, places, where_at),
        out_shape=[part, part],
        in_specs=[whole_vmem] * (1 + len(pieces)),
        out_specs=[whole_vmem] * 2,
        scratch_shapes=[
            pltpu.VMEM((width, LANES), jnp.float32),
            pltpu.VMEM((2, width + 2 * margin, LANES), jnp.float32),
            pltpu.VMEM((2, width + half, LANES), jnp.float32),
        ],
        compiler_params=pltpu.CompilerParams(vmem_limit_bytes=SUM_BYTES),
        cost_estimate=pl.CostEstimate(
            flops=8 * half * width * LANES, bytes_accessed=4 * half * slab_rows * LANES, transcendentals=0
        ),
        name="sum_lags",
    )(slabs, *pieces)


def cut_kernel(*refs):
    half = len(refs) // 3
    strip = lax.axis_index("strip")
    for index, field_ref in enumerate(refs[:half]):
        near_ref, far_ref = refs[half + 2 * index : half + 2 * index + 2]
        snaps = field_ref.shape[0]
        count, _, lanes = near_ref.shape
        depth = lanes // snaps
        for at in range(count):
            for out_ref, side in ((far_ref, 1), (near_ref, 0)):
                first = pl.multiple_of((strip ^ (2 * at + side)) * depth, depth)
                rows = [field_ref[s, pl.ds(first, depth)] for s in range(snaps)]
                out_ref[at] = jnp.concatenate(rows, 0).T


def pack_kernel(fields, *refs):
    near, far, out = refs[:fields], refs[fields : 2 * fields], refs[2 * fields :]
    distances = len(out) // fields
    for f in range(fields):
        for at in range(distances):
            out[f * distances + at][0] = near[f][at + 1]
            out[f * distances + at][1] = far[f][at + 1]


def fields_by_rows(fields):
    count = lax.axis_size("strip")
    snaps, all_rows, columns = fields[0].shape
    depth = all_rows // count
    if columns != LANES or count & (count - 1) or count < 4:
        whole = []
        for field in fields:
            cut = field.reshape(snaps, count, depth, columns).transpose(1, 3, 0, 2)
            cut = lax.all_to_all(cut.reshape(count, columns, snaps * depth), "strip", 0, 0, tiled=True)
            whole.append([cut.reshape(count * columns, snaps * depth)])
        return whole, None
    number = len(fields)
    cut = jax.ShapeDtypeStruct((count // 2, columns, snaps * depth), jnp.float32)
    parts = pl.pallas_call(
        cut_kernel,
        out_shape=[cut] * (2 * number),
        in_specs=[whole_vmem] * number,
        out_specs=[whole_vmem] * (2 * number),
        compiler_params=pltpu.CompilerParams(vmem_limit_bytes=SMALL_BYTES),
        name="cut_fields",
    )(*fields)

    def swap(part, distance):
        return lax.ppermute(part, "strip", [(i, i ^ distance) for i in range(count)])

    near, far = parts[0::2], [swap(part, 1) for part in parts[1::2]]
    distances = count // 2 - 1
    pair = jax.ShapeDtypeStruct((2, columns, snaps * depth), jnp.float32)
    packed = pl.pallas_call(
        functools.partial(pack_kernel, number),
        out_shape=[pair] * (distances * number),
        in_specs=[whole_vmem] * (2 * number),
        out_specs=[whole_vmem] * (distances * number),
        compiler_params=pltpu.CompilerParams(vmem_limit_bytes=SMALL_BYTES),
        name="pack_fields",
    )(*near, *far)
    where_at = [(0, 0, 0), (1, 0, 1)]
    where_at += [(2 + at, side, 2 * at + 2 + side) for at in range(distances) for side in range(2)]
    whole = []
    for f in range(number):
        sent = [swap(packed[f * distances + at], 2 * at + 2) for at in range(distances)]
        whole.append([near[f], far[f], *sent])
    return whole, where_at


def exchange(parts, distance):
    count = lax.axis_size("lag")
    return lax.ppermute(parts, "lag", [(i, i ^ distance) for i in range(count)])


def turn_back_kernel(first_ref, second_ref, out_ref):
    snaps, depth, _ = out_ref.shape
    for at in range(first_ref.shape[0] // LANES):
        rows = pl.ds(at * LANES, LANES)
        turned = (first_ref[rows] + second_ref[rows]).T
        for snap in range(snaps):
            out_ref[snap, :, rows] = turned[snap * depth : (snap + 1) * depth]


def sum_places(keep, send, snaps):
    both = keep + exchange(send, 1)
    rows, lanes = both.shape[1:]
    return pl.pallas_call(
        turn_back_kernel,
        out_shape=jax.ShapeDtypeStruct((snaps, lanes // snaps, rows), jnp.float32),
        in_specs=[whole_vmem] * 2,
        out_specs=whole_vmem,
        compiler_params=pltpu.CompilerParams(vmem_limit_bytes=SMALL_BYTES),
        name="turn_back",
    )(both[0], exchange(both[1], 3))


def local(image_grad, source_field, receiver_field):
    lag_count, depth, width = image_grad.shape
    snaps = source_field.shape[0]
    pad = lax.axis_size("lag") * lag_count // 2
    (receiver, source), where_at = fields_by_rows([receiver_field, source_field])
    above = chain_halo(image_grad[:, depth - 1 :], "strip", 1)
    below = chain_halo(image_grad[:, :1], "strip", -1)
    slabs = filter_slabs(image_grad, above, below, pad)
    source_adjoint = sum_places(*sum_lags(1, slabs, receiver, where_at, width), snaps)
    receiver_adjoint = sum_places(*sum_lags(-1, slabs, source, where_at, width), snaps)
    return source_adjoint, receiver_adjoint


def solution(mesh):
    in_specs = (P("lag", "strip", None), P(None, None, "strip"), P(None, None, "strip"))
    out_specs = (P(None, "strip", "lag"), P(None, "strip", "lag"))
    return jax.shard_map(local, mesh=mesh, in_specs=in_specs, out_specs=out_specs, check_vma=False)
```

```python
import functools

import jax
import jax.numpy as jnp
from jax import lax
from jax.experimental import pallas as pl
from jax.experimental.pallas import tpu as pltpu
from jax.sharding import PartitionSpec as P

LANES = 128
ROWS = 8
CLASSES = 4
PAIRS = 4
GROUPS = ((0,), (1,))
FILTER_COST = 10**9
FIRST_COST = 0
SECOND_COST = 10**9
FILTER_BYTES = 24 * 1024 * 1024
SUM_BYTES = 8 * 1024 * 1024
SMALL_BYTES = 4 * 1024 * 1024

def weight(size):
    return pl.CostEstimate(flops=size, bytes_accessed=size, transcendentals=0)


def in_hbm(array):
    return pltpu.with_memory_space_constraint(array, pltpu.HBM)


whole_vmem = pl.BlockSpec(memory_space=pltpu.VMEM)


def filter_kernel(pad, grad_hbm, near_ref, next_ref, out_ref, edges, *turned):
    lag_count, depth, width = grad_hbm.shape
    half = lag_count // 2
    tiles = width // LANES
    centers, uprights = turned[:PAIRS], turned[PAIRS:]
    core = lax.rem(lax.axis_index("strip"), 2)
    edges[1 - core] = near_ref[pl.ds(0, lag_count * tiles)]
    edges[core] = next_ref[...]
    out_ref[:, pl.ds(0, pad)] = jnp.zeros((half, pad, LANES), jnp.float32)
    out_ref[:, pl.ds(pad + width, pad)] = jnp.zeros((half, pad, LANES), jnp.float32)
    for center_t in centers:
        center_t[pl.ds(0, ROWS)] = jnp.zeros((ROWS, LANES), jnp.float32)
        center_t[pl.ds(ROWS + width, ROWS)] = jnp.zeros((ROWS, LANES), jnp.float32)

    def body(low_ref, high_ref):
        step = pl.program_id(0)
        row = lax.broadcasted_iota(jnp.int32, (depth, LANES), 0)

        def turn(within, t):
            lanes = pl.ds(t * LANES, LANES)
            mids, stencils = [], []
            for slab, shift in ((low_ref, 0), (high_ref, half)):
                lag = step * PAIRS + within + shift
                mid = slab[within, :, lanes]
                up = jnp.where(row == 0, edges[0, pl.ds(lag + t * lag_count, 1)], pltpu.roll(mid, 1, 0))
                down = jnp.where(row == depth - 1, edges[1, pl.ds(lag + t * lag_count, 1)], pltpu.roll(mid, depth - 1, 0))
                mids.append(mid)
                stencils.append(2.0 * mid - 0.25 * (up + down))
            centers[within][pl.ds(ROWS + t * LANES, LANES)] = jnp.concatenate(mids, 0).T
            uprights[within][pl.ds(t * LANES, LANES)] = jnp.concatenate(stencils, 0).T

        def join(within, t):
            west = centers[within][pl.ds(ROWS - 1 + t * LANES, LANES)]
            east = centers[within][pl.ds(ROWS + 1 + t * LANES, LANES)]
            upright = uprights[within][pl.ds(t * LANES, LANES)]
            out_ref[step * PAIRS + within, pl.ds(pad + t * LANES, LANES)] = upright - 0.25 * (west + east)

        for within in range(PAIRS + 1):
            for t in range(tiles):
                if within < PAIRS:
                    turn(within, t)
                if within:
                    join(within - 1, t)

    pltpu.emit_pipeline(
        body,
        grid=(half // PAIRS,),
        in_specs=[
            pl.BlockSpec((PAIRS, depth, width), lambda i: (i, 0, 0)),
            pl.BlockSpec((PAIRS, depth, width), lambda i: (i + half // PAIRS, 0, 0)),
        ],
        out_specs=[],
    )(grad_hbm, grad_hbm)


def filter_slabs(image_grad, from_near, from_next, pad):
    lag_count, depth, width = image_grad.shape
    return pl.pallas_call(
        functools.partial(filter_kernel, pad),
        out_shape=jax.ShapeDtypeStruct((lag_count // 2, width + 2 * pad, 2 * depth), jnp.float32),
        in_specs=[pl.BlockSpec(memory_space=pltpu.HBM), whole_vmem, whole_vmem],
        out_specs=whole_vmem,
        scratch_shapes=[pltpu.VMEM((2, *from_next.shape), jnp.float32)]
        + [pltpu.VMEM((width + 2 * ROWS, LANES), jnp.float32)] * PAIRS
        + [pltpu.VMEM((width, LANES), jnp.float32)] * PAIRS,
        compiler_params=pltpu.CompilerParams(vmem_limit_bytes=FILTER_BYTES),
        cost_estimate=weight(FILTER_COST),
        name="filter_slabs",
    )(in_hbm(image_grad), from_near, from_next)


def sum_kernel(sign, places, where_at, slab_ref, *refs):
    pieces, (keep_ref, send_ref, field_ref, paired, acc) = refs[:-5], refs[-5:]
    half, slab_rows, _ = slab_ref.shape
    width = field_ref.shape[0]
    if where_at is None:
        field_ref[...] = pieces[0][...]
    else:
        strip = lax.axis_index("strip")
        for index, row, distance in where_at:
            rows = pl.multiple_of((strip ^ distance) * LANES, LANES)
            field_ref[pl.ds(rows, LANES)] = pieces[index][pl.ds(row, LANES)]
    pad = (slab_rows - width) // 2
    lag_count = 2 * half
    margin = 2 * pad + 2 * half
    place = lax.axis_index("lag")
    first = place * lag_count - pad
    spread = width + half
    block_rows = ROWS * max(m for m in range(1, 11) if spread // ROWS % m == 0)
    low_at = 0 if sign > 0 else half
    high_at = half - low_at

    for snap in range(2):
        blank = jnp.zeros((margin + half, LANES), jnp.float32)
        paired[snap, pl.ds(0, margin)] = blank[:margin]
        paired[snap, pl.ds(margin + width, margin)] = blank[:margin]
    low = lax.broadcasted_iota(jnp.int32, (LANES, LANES), 1) < LANES // 2
    edge = jnp.zeros((half, LANES), jnp.float32)
    field = field_ref[...]
    lower = lax.broadcasted_iota(jnp.int32, (spread, LANES), 1) < LANES // 2
    if sign > 0:
        here = jnp.concatenate([edge, field], 0)
        there = jnp.concatenate([field, edge], 0)
        start = margin - half
    else:
        here = jnp.concatenate([field, edge], 0)
        there = jnp.concatenate([edge, field], 0)
        start = margin
    paired[0, pl.ds(start, spread)] = jnp.where(lower, here, pltpu.roll(there, LANES // 2, 1))
    paired[1, pl.ds(start, spread)] = jnp.where(lower, pltpu.roll(here, LANES // 2, 1), there)

    tall = block_rows // ROWS
    per_class = half // CLASSES

    def block(at, carry):
        y = at * block_rows - low_at
        slab_at = pl.multiple_of(pad + y + sign * first, ROWS)
        field_at = pl.multiple_of(margin + y + sign * 2 * first, ROWS)
        totals = [[None] * tall for _ in range(2)]
        for cls in range(CLASSES):
            held = {}
            for step in range(per_class):
                lag = step * CLASSES + cls
                for up in range(tall):
                    slab = slab_ref[lag, pl.ds(slab_at + sign * lag + up * ROWS, ROWS)]
                    for snap in range(2):
                        row = sign * 2 * lag + up * ROWS
                        if (snap, row) not in held:
                            held[snap, row] = paired[snap, pl.ds(field_at + row, ROWS)]
                        term = slab * held[snap, row]
                        total = totals[snap][up]
                        totals[snap][up] = term if total is None else total + term
        for snap in range(2):
            for up in range(tall):
                rows = pl.multiple_of(at * block_rows + up * ROWS, ROWS)
                acc[snap, pl.ds(rows, ROWS)] = totals[snap][up]
        return carry

    lax.fori_loop(0, spread // block_rows, block, 0)

    part = width // places

    def finish(target, slot, source):
        for piece in range(part // LANES):
            x = pl.multiple_of(source * part + piece * LANES, LANES)
            at_low = pl.ds(x + low_at, LANES)
            at_high = pl.ds(x + high_at, LANES)
            straight = jnp.where(low, acc[0, at_low], acc[1, at_high])
            crossed = jnp.where(low, acc[1, at_low], acc[0, at_high])
            target[slot, pl.ds(piece * LANES, LANES)] = straight + pltpu.roll(crossed, LANES // 2, 1)

    other = place + 1 - 2 * lax.rem(place, 2)
    finish(send_ref, 0, other)
    finish(send_ref, 1, places - 1 - other)
    finish(keep_ref, 0, place)
    finish(keep_ref, 1, places - 1 - place)


def sum_lags(sign, slabs, pieces, where_at, width):
    half, slab_rows, _ = slabs.shape
    pad = (slab_rows - width) // 2
    margin = 2 * pad + 2 * half
    places = lax.axis_size("lag")
    part = jax.ShapeDtypeStruct((2, width // places, LANES), jnp.float32)
    return pl.pallas_call(
        functools.partial(sum_kernel, sign, places, where_at),
        out_shape=[part, part],
        in_specs=[whole_vmem] * (1 + len(pieces)),
        out_specs=[whole_vmem] * 2,
        scratch_shapes=[
            pltpu.VMEM((width, LANES), jnp.float32),
            pltpu.VMEM((2, width + 2 * margin, LANES), jnp.float32),
            pltpu.VMEM((2, width + half, LANES), jnp.float32),
        ],
        compiler_params=pltpu.CompilerParams(vmem_limit_bytes=SUM_BYTES),
        cost_estimate=weight(FIRST_COST if sign > 0 else SECOND_COST),
        name="sum_lags",
    )(slabs, *pieces)


def send_kernel(pieces, grad_hbm, *refs):
    lag_count, depth, width = grad_hbm.shape
    tiles = width // LANES
    number = (len(refs) - 4) // 3
    fields, near_ref, next_ref = refs[:number], refs[number], refs[number + 1]
    mine = refs[number + 2 : 2 * number + 2]
    held, edges, sems = refs[2 * number + 2 : 3 * number + 2], refs[-2], refs[-1]
    strip = lax.axis_index("strip")
    core = lax.rem(strip, 2)
    copies = []
    for side in range(2):
        rows = pl.ds(side * (depth - ROWS), ROWS)
        copies.append(pltpu.make_async_copy(grad_hbm.at[:, rows], edges.at[side], sems.at[side]))
    for f in range(number):
        copies.append(pltpu.make_async_copy(fields[f], held[f], sems.at[2 + f]))
    for copy in copies:
        copy.start()

    for f in range(number):
        copies[2 + f].wait()
        snaps = held[f].shape[0]
        for at in range(pieces):
            for side in range(2):
                first = pl.multiple_of((strip ^ (2 * at + side)) * depth, depth)
                rows = [held[f][s, pl.ds(first, depth)] for s in range(snaps)]
                piece = jnp.concatenate(rows, 0).T
                if side:
                    start = lag_count * tiles + (f * pieces + at) * LANES
                    near_ref[pl.ds(start, LANES)] = piece
                else:
                    mine[f][pl.ds(at * LANES, LANES)] = piece

    copies[0].wait()
    copies[1].wait()
    low = core == 0
    for t in range(tiles):
        lanes = pl.ds(t * LANES, LANES)
        top = edges[0, :, 0, lanes]
        bottom = edges[1, :, ROWS - 1, lanes]
        rows = pl.ds(t * lag_count, lag_count)
        near_ref[rows] = jnp.where(low, bottom, top)
        next_ref[rows] = jnp.where(low, top, bottom)


def pack_kernel(pieces, edge_rows, groups, *refs):
    number = sum(len(group) for group in groups)
    mine, near_ref, out = refs[:number], refs[number], refs[number + 1 :]
    for g, group in enumerate(groups):
        for at in range(1, pieces):
            out_ref = out[g * (pieces - 1) + at - 1]
            for place, f in enumerate(group):
                rows = pl.ds(at * LANES, LANES)
                out_ref[pl.ds(2 * place * LANES, LANES)] = mine[f][rows]
                far = pl.ds(edge_rows + (f * pieces + at) * LANES, LANES)
                out_ref[pl.ds((2 * place + 1) * LANES, LANES)] = near_ref[far]


def strip_swap(part, distance):
    count = lax.axis_size("strip")
    return lax.ppermute(part, "strip", [(i, i ^ distance) for i in range(count)])


def gather_rows(image_grad, fields):
    lag_count, depth, width = image_grad.shape
    count = lax.axis_size("strip")
    snaps, all_rows, columns = fields[0].shape
    direct = columns == LANES and count >= 4 and count & (count - 1) == 0
    pieces = count // 2 if direct else 0
    number = len(fields) if direct else 0
    edge_rows = lag_count * (width // LANES)

    def buffer(rows):
        return jax.ShapeDtypeStruct((rows, LANES), jnp.float32)

    near, following, *mine = pl.pallas_call(
        functools.partial(send_kernel, pieces),
        out_shape=[buffer(edge_rows + number * pieces * LANES), buffer(edge_rows)]
        + [buffer(pieces * LANES)] * number,
        in_specs=[pl.BlockSpec(memory_space=pltpu.HBM)] * (1 + number),
        out_specs=[whole_vmem] * (2 + number),
        scratch_shapes=[pltpu.VMEM(f.shape, jnp.float32) for f in fields[:number]]
        + [pltpu.VMEM((2, lag_count, ROWS, width), jnp.float32), pltpu.SemaphoreType.DMA((2 + number,))],
        compiler_params=pltpu.CompilerParams(vmem_limit_bytes=SUM_BYTES),
        name="send_rows",
    )(*(in_hbm(a) for a in (image_grad, *fields[:number])))
    near = strip_swap(near, 1)
    following = lax.ppermute(
        following, "strip", [p for i in range(1, count - 1, 2) for p in ((i, i + 1), (i + 1, i))]
    )
    if not direct:
        whole = []
        for field in fields:
            cut = field.reshape(snaps, count, depth, columns).transpose(1, 3, 0, 2)
            cut = lax.all_to_all(cut.reshape(count, columns, snaps * depth), "strip", 0, 0, tiled=True)
            whole.append([cut.reshape(count * columns, snaps * depth)])
        return near, following, whole, [None] * len(fields)

    out_shape = [buffer(2 * len(group) * LANES) for group in GROUPS for at in range(1, pieces)]
    packed = pl.pallas_call(
        functools.partial(pack_kernel, pieces, edge_rows, GROUPS),
        out_shape=out_shape,
        in_specs=[whole_vmem] * (number + 1),
        out_specs=[whole_vmem] * len(out_shape),
        compiler_params=pltpu.CompilerParams(vmem_limit_bytes=SMALL_BYTES),
        name="pack_fields",
    )(*mine, near)
    whole, where_at = [None] * number, [None] * number
    for g, group in enumerate(GROUPS):
        sent = [strip_swap(packed[g * (pieces - 1) + at - 1], 2 * at) for at in range(1, pieces)]
        for place, f in enumerate(group):
            whole[f] = [mine[f], near, *sent]
            where_at[f] = [(0, 0, 0), (1, edge_rows + f * pieces * LANES, 1)]
            where_at[f] += [
                (1 + at, (2 * place + side) * LANES, 2 * at + side) for at in range(1, pieces) for side in range(2)
            ]
    return near, following, whole, where_at


def exchange(parts, distance):
    count = lax.axis_size("lag")
    return lax.ppermute(parts, "lag", [(i, i ^ distance) for i in range(count)])


def turn_back_kernel(first_ref, second_ref, out_ref):
    snaps, depth, _ = out_ref.shape
    for at in range(first_ref.shape[0] // LANES):
        rows = pl.ds(at * LANES, LANES)
        turned = (first_ref[rows] + second_ref[rows]).T
        for snap in range(snaps):
            out_ref[snap, :, rows] = turned[snap * depth : (snap + 1) * depth]


def sum_places(keep, send, snaps):
    both = keep + exchange(send, 1)
    rows, lanes = both.shape[1:]
    return pl.pallas_call(
        turn_back_kernel,
        out_shape=jax.ShapeDtypeStruct((snaps, lanes // snaps, rows), jnp.float32),
        in_specs=[whole_vmem] * 2,
        out_specs=whole_vmem,
        compiler_params=pltpu.CompilerParams(vmem_limit_bytes=SMALL_BYTES),
        name="turn_back",
    )(both[0], exchange(both[1], 3))


def local(image_grad, source_field, receiver_field):
    lag_count, depth, width = image_grad.shape
    snaps = source_field.shape[0]
    pad = lax.axis_size("lag") * lag_count // 2
    near, following, (receiver, source), (at_first, at_second) = gather_rows(
        image_grad, [receiver_field, source_field]
    )
    slabs = filter_slabs(image_grad, near, following, pad)
    source_adjoint = sum_places(*sum_lags(1, slabs, receiver, at_first, width), snaps)
    receiver_adjoint = sum_places(*sum_lags(-1, slabs, source, at_second, width), snaps)
    return source_adjoint, receiver_adjoint


def solution(mesh):
    in_specs = (P("lag", "strip", None), P(None, None, "strip"), P(None, None, "strip"))
    out_specs = (P(None, "strip", "lag"), P(None, "strip", "lag"))
    return jax.shard_map(local, mesh=mesh, in_specs=in_specs, out_specs=out_specs, check_vma=False)
```

```python
import functools

import jax
import jax.numpy as jnp
from jax import lax
from jax.experimental import pallas as pl
from jax.experimental.pallas import tpu as pltpu
from jax.sharding import PartitionSpec as P

LANES = 128
ROWS = 8
CLASSES = 4
PAIRS = 4
GROUPS = ((0, 1),)
FILTER_COST = 3 * 10**9
FIRST_COST = 0
SECOND_COST = 10**9
FILTER_BYTES = 24 * 1024 * 1024
SUM_BYTES = 8 * 1024 * 1024
SMALL_BYTES = 4 * 1024 * 1024

def weight(size):
    return pl.CostEstimate(flops=size, bytes_accessed=size, transcendentals=0)


def in_hbm(array):
    return pltpu.with_memory_space_constraint(array, pltpu.HBM)


whole_vmem = pl.BlockSpec(memory_space=pltpu.VMEM)


def filter_kernel(pad, grad_hbm, near_ref, next_ref, out_ref, edges, *turned):
    lag_count, depth, width = grad_hbm.shape
    half = lag_count // 2
    tiles = width // LANES
    centers, uprights = turned[:PAIRS], turned[PAIRS:]
    core = lax.rem(lax.axis_index("strip"), 2)
    edges[1 - core] = near_ref[pl.ds(0, lag_count * tiles)]
    edges[core] = next_ref[...]
    out_ref[:, pl.ds(0, pad)] = jnp.zeros((half, pad, LANES), jnp.float32)
    out_ref[:, pl.ds(pad + width, pad)] = jnp.zeros((half, pad, LANES), jnp.float32)
    for center_t in centers:
        center_t[pl.ds(0, ROWS)] = jnp.zeros((ROWS, LANES), jnp.float32)
        center_t[pl.ds(ROWS + width, ROWS)] = jnp.zeros((ROWS, LANES), jnp.float32)

    def body(low_ref, high_ref):
        step = pl.program_id(0)
        row = lax.broadcasted_iota(jnp.int32, (depth, LANES), 0)

        def turn(within, t):
            lanes = pl.ds(t * LANES, LANES)
            mids, stencils = [], []
            for slab, shift in ((low_ref, 0), (high_ref, half)):
                lag = step * PAIRS + within + shift
                mid = slab[within, :, lanes]
                up = jnp.where(row == 0, edges[0, pl.ds(lag + t * lag_count, 1)], pltpu.roll(mid, 1, 0))
                down = jnp.where(row == depth - 1, edges[1, pl.ds(lag + t * lag_count, 1)], pltpu.roll(mid, depth - 1, 0))
                mids.append(mid)
                stencils.append(2.0 * mid - 0.25 * (up + down))
            centers[within][pl.ds(ROWS + t * LANES, LANES)] = jnp.concatenate(mids, 0).T
            uprights[within][pl.ds(t * LANES, LANES)] = jnp.concatenate(stencils, 0).T

        def join(within, t):
            west = centers[within][pl.ds(ROWS - 1 + t * LANES, LANES)]
            east = centers[within][pl.ds(ROWS + 1 + t * LANES, LANES)]
            upright = uprights[within][pl.ds(t * LANES, LANES)]
            out_ref[step * PAIRS + within, pl.ds(pad + t * LANES, LANES)] = upright - 0.25 * (west + east)

        for within in range(PAIRS + 1):
            for t in range(tiles):
                if within < PAIRS:
                    turn(within, t)
                if within:
                    join(within - 1, t)

    pltpu.emit_pipeline(
        body,
        grid=(half // PAIRS,),
        in_specs=[
            pl.BlockSpec((PAIRS, depth, width), lambda i: (i, 0, 0)),
            pl.BlockSpec((PAIRS, depth, width), lambda i: (i + half // PAIRS, 0, 0)),
        ],
        out_specs=[],
    )(grad_hbm, grad_hbm)


def filter_slabs(image_grad, from_near, from_next, pad):
    lag_count, depth, width = image_grad.shape
    return pl.pallas_call(
        functools.partial(filter_kernel, pad),
        out_shape=jax.ShapeDtypeStruct((lag_count // 2, width + 2 * pad, 2 * depth), jnp.float32),
        in_specs=[pl.BlockSpec(memory_space=pltpu.HBM), whole_vmem, whole_vmem],
        out_specs=whole_vmem,
        scratch_shapes=[pltpu.VMEM((2, *from_next.shape), jnp.float32)]
        + [pltpu.VMEM((width + 2 * ROWS, LANES), jnp.float32)] * PAIRS
        + [pltpu.VMEM((width, LANES), jnp.float32)] * PAIRS,
        compiler_params=pltpu.CompilerParams(vmem_limit_bytes=FILTER_BYTES),
        cost_estimate=weight(FILTER_COST),
        name="filter_slabs",
    )(in_hbm(image_grad), from_near, from_next)


def sum_kernel(sign, places, where_at, slab_ref, *refs):
    pieces, (keep_ref, send_ref, field_ref, paired, acc) = refs[:-5], refs[-5:]
    half, slab_rows, _ = slab_ref.shape
    width = field_ref.shape[0]
    if where_at is None:
        field_ref[...] = pieces[0][...]
    else:
        strip = lax.axis_index("strip")
        for index, row, distance in where_at:
            rows = pl.multiple_of((strip ^ distance) * LANES, LANES)
            field_ref[pl.ds(rows, LANES)] = pieces[index][pl.ds(row, LANES)]
    pad = (slab_rows - width) // 2
    lag_count = 2 * half
    margin = 2 * pad + 2 * half
    place = lax.axis_index("lag")
    first = place * lag_count - pad
    spread = width + half
    block_rows = ROWS * max(m for m in range(1, 11) if spread // ROWS % m == 0)
    low_at = 0 if sign > 0 else half
    high_at = half - low_at

    for snap in range(2):
        blank = jnp.zeros((margin + half, LANES), jnp.float32)
        paired[snap, pl.ds(0, margin)] = blank[:margin]
        paired[snap, pl.ds(margin + width, margin)] = blank[:margin]
    low = lax.broadcasted_iota(jnp.int32, (LANES, LANES), 1) < LANES // 2
    edge = jnp.zeros((half, LANES), jnp.float32)
    field = field_ref[...]
    lower = lax.broadcasted_iota(jnp.int32, (spread, LANES), 1) < LANES // 2
    if sign > 0:
        here = jnp.concatenate([edge, field], 0)
        there = jnp.concatenate([field, edge], 0)
        start = margin - half
    else:
        here = jnp.concatenate([field, edge], 0)
        there = jnp.concatenate([edge, field], 0)
        start = margin
    paired[0, pl.ds(start, spread)] = jnp.where(lower, here, pltpu.roll(there, LANES // 2, 1))
    paired[1, pl.ds(start, spread)] = jnp.where(lower, pltpu.roll(here, LANES // 2, 1), there)

    tall = block_rows // ROWS
    per_class = half // CLASSES

    def block(at, carry):
        y = at * block_rows - low_at
        slab_at = pl.multiple_of(pad + y + sign * first, ROWS)
        field_at = pl.multiple_of(margin + y + sign * 2 * first, ROWS)
        totals = [[None] * tall for _ in range(2)]
        for cls in range(CLASSES):
            held = {}
            for step in range(per_class):
                lag = step * CLASSES + cls
                for up in range(tall):
                    slab = slab_ref[lag, pl.ds(slab_at + sign * lag + up * ROWS, ROWS)]
                    for snap in range(2):
                        row = sign * 2 * lag + up * ROWS
                        if (snap, row) not in held:
                            held[snap, row] = paired[snap, pl.ds(field_at + row, ROWS)]
                        term = slab * held[snap, row]
                        total = totals[snap][up]
                        totals[snap][up] = term if total is None else total + term
        for snap in range(2):
            for up in range(tall):
                rows = pl.multiple_of(at * block_rows + up * ROWS, ROWS)
                acc[snap, pl.ds(rows, ROWS)] = totals[snap][up]
        return carry

    lax.fori_loop(0, spread // block_rows, block, 0)

    part = width // places

    def finish(target, slot, source):
        for piece in range(part // LANES):
            x = pl.multiple_of(source * part + piece * LANES, LANES)
            at_low = pl.ds(x + low_at, LANES)
            at_high = pl.ds(x + high_at, LANES)
            straight = jnp.where(low, acc[0, at_low], acc[1, at_high])
            crossed = jnp.where(low, acc[1, at_low], acc[0, at_high])
            target[slot, pl.ds(piece * LANES, LANES)] = straight + pltpu.roll(crossed, LANES // 2, 1)

    other = place + 1 - 2 * lax.rem(place, 2)
    finish(send_ref, 0, other)
    finish(send_ref, 1, places - 1 - other)
    finish(keep_ref, 0, place)
    finish(keep_ref, 1, places - 1 - place)


def sum_lags(sign, slabs, pieces, where_at, width):
    half, slab_rows, _ = slabs.shape
    pad = (slab_rows - width) // 2
    margin = 2 * pad + 2 * half
    places = lax.axis_size("lag")
    part = jax.ShapeDtypeStruct((2, width // places, LANES), jnp.float32)
    return pl.pallas_call(
        functools.partial(sum_kernel, sign, places, where_at),
        out_shape=[part, part],
        in_specs=[whole_vmem] * (1 + len(pieces)),
        out_specs=[whole_vmem] * 2,
        scratch_shapes=[
            pltpu.VMEM((width, LANES), jnp.float32),
            pltpu.VMEM((2, width + 2 * margin, LANES), jnp.float32),
            pltpu.VMEM((2, width + half, LANES), jnp.float32),
        ],
        compiler_params=pltpu.CompilerParams(vmem_limit_bytes=SUM_BYTES),
        cost_estimate=weight(FIRST_COST if sign > 0 else SECOND_COST),
        name="sum_lags",
    )(slabs, *pieces)


def send_kernel(pieces, grad_hbm, *refs):
    lag_count, depth, width = grad_hbm.shape
    tiles = width // LANES
    number = (len(refs) - 4) // 3
    fields, near_ref, next_ref = refs[:number], refs[number], refs[number + 1]
    mine = refs[number + 2 : 2 * number + 2]
    held, edges, sems = refs[2 * number + 2 : 3 * number + 2], refs[-2], refs[-1]
    strip = lax.axis_index("strip")
    core = lax.rem(strip, 2)
    copies = []
    for side in range(2):
        rows = pl.ds(side * (depth - ROWS), ROWS)
        copies.append(pltpu.make_async_copy(grad_hbm.at[:, rows], edges.at[side], sems.at[side]))
    for f in range(number):
        copies.append(pltpu.make_async_copy(fields[f], held[f], sems.at[2 + f]))
    for copy in copies:
        copy.start()

    for f in range(number):
        copies[2 + f].wait()
        snaps = held[f].shape[0]
        for at in range(pieces):
            for side in range(2):
                first = pl.multiple_of((strip ^ (2 * at + side)) * depth, depth)
                rows = [held[f][s, pl.ds(first, depth)] for s in range(snaps)]
                piece = jnp.concatenate(rows, 0).T
                if side:
                    start = lag_count * tiles + (f * pieces + at) * LANES
                    near_ref[pl.ds(start, LANES)] = piece
                else:
                    mine[f][pl.ds(at * LANES, LANES)] = piece

    copies[0].wait()
    copies[1].wait()
    low = core == 0
    for t in range(tiles):
        lanes = pl.ds(t * LANES, LANES)
        top = edges[0, :, 0, lanes]
        bottom = edges[1, :, ROWS - 1, lanes]
        rows = pl.ds(t * lag_count, lag_count)
        near_ref[rows] = jnp.where(low, bottom, top)
        next_ref[rows] = jnp.where(low, top, bottom)


def pack_kernel(pieces, edge_rows, groups, *refs):
    number = sum(len(group) for group in groups)
    mine, near_ref, out = refs[:number], refs[number], refs[number + 1 :]
    for g, group in enumerate(groups):
        for at in range(1, pieces):
            out_ref = out[g * (pieces - 1) + at - 1]
            for place, f in enumerate(group):
                rows = pl.ds(at * LANES, LANES)
                out_ref[pl.ds(2 * place * LANES, LANES)] = mine[f][rows]
                far = pl.ds(edge_rows + (f * pieces + at) * LANES, LANES)
                out_ref[pl.ds((2 * place + 1) * LANES, LANES)] = near_ref[far]


def strip_swap(part, distance):
    count = lax.axis_size("strip")
    return lax.ppermute(part, "strip", [(i, i ^ distance) for i in range(count)])


def gather_rows(image_grad, fields):
    lag_count, depth, width = image_grad.shape
    count = lax.axis_size("strip")
    snaps, all_rows, columns = fields[0].shape
    direct = columns == LANES and count >= 4 and count & (count - 1) == 0
    pieces = count // 2 if direct else 0
    number = len(fields) if direct else 0
    edge_rows = lag_count * (width // LANES)

    def buffer(rows):
        return jax.ShapeDtypeStruct((rows, LANES), jnp.float32)

    near, following, *mine = pl.pallas_call(
        functools.partial(send_kernel, pieces),
        out_shape=[buffer(edge_rows + number * pieces * LANES), buffer(edge_rows)]
        + [buffer(pieces * LANES)] * number,
        in_specs=[pl.BlockSpec(memory_space=pltpu.HBM)] * (1 + number),
        out_specs=[whole_vmem] * (2 + number),
        scratch_shapes=[pltpu.VMEM(f.shape, jnp.float32) for f in fields[:number]]
        + [pltpu.VMEM((2, lag_count, ROWS, width), jnp.float32), pltpu.SemaphoreType.DMA((2 + number,))],
        compiler_params=pltpu.CompilerParams(vmem_limit_bytes=SUM_BYTES),
        name="send_rows",
    )(*(in_hbm(a) for a in (image_grad, *fields[:number])))
    near = strip_swap(near, 1)
    following = lax.ppermute(
        following, "strip", [p for i in range(1, count - 1, 2) for p in ((i, i + 1), (i + 1, i))]
    )
    if not direct:
        whole = []
        for field in fields:
            cut = field.reshape(snaps, count, depth, columns).transpose(1, 3, 0, 2)
            cut = lax.all_to_all(cut.reshape(count, columns, snaps * depth), "strip", 0, 0, tiled=True)
            whole.append([cut.reshape(count * columns, snaps * depth)])
        return near, following, whole, [None] * len(fields)

    out_shape = [buffer(2 * len(group) * LANES) for group in GROUPS for at in range(1, pieces)]
    packed = pl.pallas_call(
        functools.partial(pack_kernel, pieces, edge_rows, GROUPS),
        out_shape=out_shape,
        in_specs=[whole_vmem] * (number + 1),
        out_specs=[whole_vmem] * len(out_shape),
        compiler_params=pltpu.CompilerParams(vmem_limit_bytes=SMALL_BYTES),
        name="pack_fields",
    )(*mine, near)
    whole, where_at = [None] * number, [None] * number
    for g, group in enumerate(GROUPS):
        sent = [strip_swap(packed[g * (pieces - 1) + at - 1], 2 * at) for at in range(1, pieces)]
        for place, f in enumerate(group):
            whole[f] = [mine[f], near, *sent]
            where_at[f] = [(0, 0, 0), (1, edge_rows + f * pieces * LANES, 1)]
            where_at[f] += [
                (1 + at, (2 * place + side) * LANES, 2 * at + side) for at in range(1, pieces) for side in range(2)
            ]
    return near, following, whole, where_at


def exchange(parts, distance):
    count = lax.axis_size("lag")
    return lax.ppermute(parts, "lag", [(i, i ^ distance) for i in range(count)])


def turn_back_kernel(first_ref, second_ref, out_ref):
    snaps, depth, _ = out_ref.shape
    for at in range(first_ref.shape[0] // LANES):
        rows = pl.ds(at * LANES, LANES)
        turned = (first_ref[rows] + second_ref[rows]).T
        for snap in range(snaps):
            out_ref[snap, :, rows] = turned[snap * depth : (snap + 1) * depth]


def sum_places(keep, send, snaps):
    both = keep + exchange(send, 1)
    rows, lanes = both.shape[1:]
    return pl.pallas_call(
        turn_back_kernel,
        out_shape=jax.ShapeDtypeStruct((snaps, lanes // snaps, rows), jnp.float32),
        in_specs=[whole_vmem] * 2,
        out_specs=whole_vmem,
        compiler_params=pltpu.CompilerParams(vmem_limit_bytes=SMALL_BYTES),
        name="turn_back",
    )(both[0], exchange(both[1], 3))


def local(image_grad, source_field, receiver_field):
    lag_count, depth, width = image_grad.shape
    snaps = source_field.shape[0]
    pad = lax.axis_size("lag") * lag_count // 2
    near, following, (receiver, source), (at_first, at_second) = gather_rows(
        image_grad, [receiver_field, source_field]
    )
    slabs = filter_slabs(image_grad, near, following, pad)
    source_adjoint = sum_places(*sum_lags(1, slabs, receiver, at_first, width), snaps)
    receiver_adjoint = sum_places(*sum_lags(-1, slabs, source, at_second, width), snaps)
    return source_adjoint, receiver_adjoint


def solution(mesh):
    in_specs = (P("lag", "strip", None), P(None, None, "strip"), P(None, None, "strip"))
    out_specs = (P(None, "strip", "lag"), P(None, "strip", "lag"))
    return jax.shard_map(local, mesh=mesh, in_specs=in_specs, out_specs=out_specs, check_vma=False)
```

```python
import functools

import jax
import jax.numpy as jnp
from jax import lax
from jax.experimental import pallas as pl
from jax.experimental.pallas import tpu as pltpu
from jax.sharding import PartitionSpec as P

LANES = 128
ROWS = 8
CLASSES = 4
PAIRS = 4
CHUNK = 512
ALONE = 1
FIRST_FORM = "direct"
SECOND_FORM = "halves"
ORDERED = True
GRAD_IN_HBM = True
FILTER_COST = 3 * 10**9
FIRST_COST = 0
SECOND_COST = 10**9
FILTER_BYTES = 32 * 1024 * 1024
SUM_BYTES = 8 * 1024 * 1024
SMALL_BYTES = 4 * 1024 * 1024

def weight(size):
    return pl.CostEstimate(flops=size, bytes_accessed=size, transcendentals=0)


def in_hbm(array):
    return pltpu.with_memory_space_constraint(array, pltpu.HBM)


whole_vmem = pl.BlockSpec(memory_space=pltpu.VMEM)


def filter_kernel(pad, grad_hbm, near_ref, next_ref, out_ref, edge_parts, held, sems, *turned):
    lag_count, depth, width = grad_hbm.shape
    half = lag_count // 2
    tiles = width // LANES
    steps = half // PAIRS

    def fetch(step, side):
        lags = pl.ds(step * PAIRS + side * half, PAIRS)
        return pltpu.make_async_copy(grad_hbm.at[lags], held.at[lags], sems.at[2 * step + side])

    for step in range(steps):
        for side in range(2):
            fetch(step, side).start()

    centers = turned
    strip = lax.axis_index("strip")
    core = lax.rem(strip, 2)
    inside = (strip != 0) & (strip != lax.axis_size("strip") - 1)
    blank = jnp.zeros((LANES - 2 * lag_count, LANES), jnp.float32)

    def split(value):
        high = value.astype(jnp.bfloat16)
        return high, (value - high.astype(jnp.float32)).astype(jnp.bfloat16)

    for t in range(tiles):
        rows = pl.ds(t * lag_count, lag_count)
        near, following = near_ref[rows], jnp.where(inside, next_ref[rows], 0.0)
        above = jnp.where(core == 0, following, near)
        below = jnp.where(core == 0, near, following)
        parts = split(jnp.concatenate([above, below, blank], 0).T)
        for part in range(2):
            edge_parts[part, pl.ds(t * LANES, LANES)] = parts[part]
    out_ref[:, pl.ds(0, pad)] = jnp.zeros((half, pad, LANES), jnp.float32)
    out_ref[:, pl.ds(pad + width, pad)] = jnp.zeros((half, pad, LANES), jnp.float32)
    for center_t in centers:
        center_t[pl.ds(0, ROWS)] = jnp.zeros((ROWS, LANES), jnp.float32)
        center_t[pl.ds(ROWS + width, ROWS)] = jnp.zeros((ROWS, LANES), jnp.float32)

    def body(step, carry):
        fetch(step, 0).wait()
        fetch(step, 1).wait()
        low_ref, high_ref = held.at[pl.ds(step * PAIRS, PAIRS)], held.at[pl.ds(step * PAIRS + half, PAIRS)]
        source = lax.broadcasted_iota(jnp.int32, (LANES, LANES), 0)
        target = lax.broadcasted_iota(jnp.int32, (LANES, LANES), 1)
        beside = (jnp.abs(source - target) == 1) & ((source < depth) == (target < depth))
        band = jnp.where(source == target, 2.0, jnp.where(beside, -0.25, 0.0))
        upper = jnp.where(target == 0, 0, jnp.where(target == depth, half, 2 * LANES))
        lower = jnp.where(target == depth - 1, 0, jnp.where(target == 2 * depth - 1, half, 2 * LANES))
        matrices = []
        for within in range(PAIRS):
            lag = step * PAIRS + within
            chosen = (source == upper + lag) | (source == lower + lag + lag_count)
            choice = jnp.where(chosen, -0.25, 0.0)
            matrices.append(jnp.concatenate([band, choice], 0).astype(jnp.bfloat16))

        def turn(within, t):
            rows = pl.ds(t * LANES, LANES)
            center = jnp.concatenate([low_ref[within, :, rows], high_ref[within, :, rows]], 0).T
            centers[within][pl.ds(ROWS + t * LANES, LANES)] = center

        def join(within, at):
            rows = pl.ds(at * chunk, chunk)
            west = centers[within][pl.ds(ROWS - 1 + at * chunk, chunk)]
            east = centers[within][pl.ds(ROWS + 1 + at * chunk, chunk)]
            parts = split(centers[within][pl.ds(ROWS + at * chunk, chunk)])
            products = [
                jnp.dot(
                    jnp.concatenate([parts[part], edge_parts[part, rows]], 1),
                    matrices[within],
                    preferred_element_type=jnp.float32,
                )
                for part in range(2)
            ]
            value = (products[0] + products[1]) - 0.25 * (west + east)
            out_ref[step * PAIRS + within, pl.ds(pad + at * chunk, chunk)] = value

        chunk = min(CHUNK, width)
        for within in range(PAIRS + 1):
            for t in range(tiles):
                if within < PAIRS:
                    turn(within, t)
                if within and (t + 1) * LANES % chunk == 0:
                    join(within - 1, ((t + 1) * LANES // chunk) - 1)
        return carry

    lax.fori_loop(0, steps, body, 0)


def filter_slabs(image_grad, from_near, from_next, pad):
    lag_count, depth, width = image_grad.shape
    return pl.pallas_call(
        functools.partial(filter_kernel, pad),
        out_shape=jax.ShapeDtypeStruct((lag_count // 2, width + 2 * pad, 2 * depth), jnp.float32),
        in_specs=[pl.BlockSpec(memory_space=pltpu.HBM if GRAD_IN_HBM else pl.ANY), whole_vmem, whole_vmem],
        out_specs=whole_vmem,
        scratch_shapes=[pltpu.VMEM((2, width, LANES), jnp.bfloat16)]
        + [pltpu.VMEM(image_grad.shape, jnp.float32), pltpu.SemaphoreType.DMA((lag_count // PAIRS,))]
        + [pltpu.VMEM((width + 2 * ROWS, LANES), jnp.float32)] * PAIRS,
        compiler_params=pltpu.CompilerParams(vmem_limit_bytes=FILTER_BYTES),
        cost_estimate=weight(FILTER_COST),
        name="filter_slabs",
    )(in_hbm(image_grad) if GRAD_IN_HBM else image_grad, from_near, from_next)


def sum_kernel(sign, places, where_at, blocks, slab_ref, *refs):
    number = len(blocks)
    pieces, outs = refs[: -3 - number], refs[-3 - number : -3]
    field_ref, paired, acc = refs[-3:]
    half, slab_rows, _ = slab_ref.shape
    width = field_ref.shape[0]
    if where_at is None:
        field_ref[...] = pieces[0][...]
    else:
        strip = lax.axis_index("strip")
        for index, row, distance in where_at:
            rows = pl.multiple_of((strip ^ distance) * LANES, LANES)
            field_ref[pl.ds(rows, LANES)] = pieces[index][pl.ds(row, LANES)]
    pad = (slab_rows - width) // 2
    lag_count = 2 * half
    margin = 2 * pad + 2 * half
    place = lax.axis_index("lag")
    first = place * lag_count - pad
    spread = width + half
    block_rows = ROWS * max(m for m in range(1, 11) if spread // ROWS % m == 0)
    low_at = 0 if sign > 0 else half
    high_at = half - low_at

    for snap in range(2):
        blank = jnp.zeros((margin + half, LANES), jnp.float32)
        paired[snap, pl.ds(0, margin)] = blank[:margin]
        paired[snap, pl.ds(margin + width, margin)] = blank[:margin]
    low = lax.broadcasted_iota(jnp.int32, (LANES, LANES), 1) < LANES // 2
    edge = jnp.zeros((half, LANES), jnp.float32)
    field = field_ref[...]
    lower = lax.broadcasted_iota(jnp.int32, (spread, LANES), 1) < LANES // 2
    if sign > 0:
        here = jnp.concatenate([edge, field], 0)
        there = jnp.concatenate([field, edge], 0)
        start = margin - half
    else:
        here = jnp.concatenate([field, edge], 0)
        there = jnp.concatenate([edge, field], 0)
        start = margin
    paired[0, pl.ds(start, spread)] = jnp.where(lower, here, pltpu.roll(there, LANES // 2, 1))
    paired[1, pl.ds(start, spread)] = jnp.where(lower, pltpu.roll(here, LANES // 2, 1), there)

    tall = block_rows // ROWS
    per_class = half // CLASSES

    def block(at, carry):
        y = at * block_rows - low_at
        slab_at = pl.multiple_of(pad + y + sign * first, ROWS)
        field_at = pl.multiple_of(margin + y + sign * 2 * first, ROWS)
        totals = [[None] * tall for _ in range(2)]
        for cls in range(CLASSES):
            held = {}
            for step in range(per_class):
                lag = step * CLASSES + cls
                for up in range(tall):
                    slab = slab_ref[lag, pl.ds(slab_at + sign * lag + up * ROWS, ROWS)]
                    for snap in range(2):
                        row = sign * 2 * lag + up * ROWS
                        if (snap, row) not in held:
                            held[snap, row] = paired[snap, pl.ds(field_at + row, ROWS)]
                        term = slab * held[snap, row]
                        total = totals[snap][up]
                        totals[snap][up] = term if total is None else total + term
        for snap in range(2):
            for up in range(tall):
                rows = pl.multiple_of(at * block_rows + up * ROWS, ROWS)
                acc[snap, pl.ds(rows, ROWS)] = totals[snap][up]
        return carry

    lax.fori_loop(0, spread // block_rows, block, 0)

    part = width // places

    def finish(target, slot, source):
        for piece in range(part // LANES):
            x = pl.multiple_of(source * part + piece * LANES, LANES)
            at_low = pl.ds(x + low_at, LANES)
            at_high = pl.ds(x + high_at, LANES)
            straight = jnp.where(low, acc[0, at_low], acc[1, at_high])
            crossed = jnp.where(low, acc[1, at_low], acc[0, at_high])
            rows = pl.ds(slot * part + piece * LANES, LANES)
            target[rows] = straight + pltpu.roll(crossed, LANES // 2, 1)

    for target, distances in zip(outs, blocks):
        for slot, distance in enumerate(distances):
            finish(target, slot, place ^ distance)


BLOCKS = {
    "direct": ((0,), (1,), (2,), (3,)),
    "halves": ((0, 3), (1, 2)),
    "forward": ((0,), (2,), (3, 1), (3,)),
}


def sum_lags(sign, form, slabs, pieces, where_at, width, after=()):
    half, slab_rows, _ = slabs.shape
    pad = (slab_rows - width) // 2
    margin = 2 * pad + 2 * half
    places = lax.axis_size("lag")
    part = width // places
    out_shape = [jax.ShapeDtypeStruct((len(held) * part, LANES), jnp.float32) for held in BLOCKS[form]]
    return pl.pallas_call(
        functools.partial(sum_kernel, sign, places, where_at, BLOCKS[form]),
        out_shape=out_shape,
        in_specs=[whole_vmem] * (1 + len(pieces) + len(after)),
        out_specs=[whole_vmem] * len(out_shape),
        scratch_shapes=[
            pltpu.VMEM((width, LANES), jnp.float32),
            pltpu.VMEM((2, width + 2 * margin, LANES), jnp.float32),
            pltpu.VMEM((2, width + half, LANES), jnp.float32),
        ],
        compiler_params=pltpu.CompilerParams(vmem_limit_bytes=SUM_BYTES),
        cost_estimate=weight(FIRST_COST if sign > 0 else SECOND_COST),
        name="sum_lags",
    )(slabs, *pieces, *after)


def send_kernel(pieces, grad_hbm, *refs):
    lag_count, depth, width = grad_hbm.shape
    tiles = width // LANES
    number = (len(refs) - 4) // 3
    fields, near_ref, next_ref = refs[:number], refs[number], refs[number + 1]
    mine = refs[number + 2 : 2 * number + 2]
    held, edges, sems = refs[2 * number + 2 : 3 * number + 2], refs[-2], refs[-1]
    strip = lax.axis_index("strip")
    core = lax.rem(strip, 2)
    copies = []
    for side in range(2):
        rows = pl.ds(side * (depth - ROWS), ROWS)
        copies.append(pltpu.make_async_copy(grad_hbm.at[:, rows], edges.at[side], sems.at[side]))
    for f in range(number):
        copies.append(pltpu.make_async_copy(fields[f], held[f], sems.at[2 + f]))
    for copy in copies:
        copy.start()

    for f in range(number):
        copies[2 + f].wait()
        snaps = held[f].shape[0]
        for at in range(pieces):
            for side in range(2):
                first = pl.multiple_of((strip ^ (2 * at + side)) * depth, depth)
                rows = [held[f][s, pl.ds(first, depth)] for s in range(snaps)]
                piece = jnp.concatenate(rows, 0).T
                if side:
                    start = lag_count * tiles + (f * pieces + at) * LANES
                    near_ref[pl.ds(start, LANES)] = piece
                else:
                    mine[f][pl.ds(at * LANES, LANES)] = piece

    copies[0].wait()
    copies[1].wait()
    low = core == 0
    for t in range(tiles):
        lanes = pl.ds(t * LANES, LANES)
        top = edges[0, :, 0, lanes]
        bottom = edges[1, :, ROWS - 1, lanes]
        rows = pl.ds(t * lag_count, lag_count)
        near_ref[rows] = jnp.where(low, bottom, top)
        next_ref[rows] = jnp.where(low, top, bottom)


def pack_kernel(pieces, edge_rows, sends, *refs):
    number = 1 + max(f for _, group in sends for f in group)
    mine, near_ref, out = refs[:number], refs[number], refs[number + 1 :]
    for (at, group), out_ref in zip(sends, out):
        for place, f in enumerate(group):
            rows = pl.ds(at * LANES, LANES)
            out_ref[pl.ds(2 * place * LANES, LANES)] = mine[f][rows]
            far = pl.ds(edge_rows + (f * pieces + at) * LANES, LANES)
            out_ref[pl.ds((2 * place + 1) * LANES, LANES)] = near_ref[far]


def strip_swap(part, distance):
    count = lax.axis_size("strip")
    return lax.ppermute(part, "strip", [(i, i ^ distance) for i in range(count)])


def gather_rows(image_grad, fields):
    lag_count, depth, width = image_grad.shape
    count = lax.axis_size("strip")
    snaps, all_rows, columns = fields[0].shape
    direct = columns == LANES and count >= 4 and count & (count - 1) == 0
    pieces = count // 2 if direct else 0
    number = len(fields) if direct else 0
    edge_rows = lag_count * (width // LANES)

    def buffer(rows):
        return jax.ShapeDtypeStruct((rows, LANES), jnp.float32)

    near, following, *mine = pl.pallas_call(
        functools.partial(send_kernel, pieces),
        out_shape=[buffer(edge_rows + number * pieces * LANES), buffer(edge_rows)]
        + [buffer(pieces * LANES)] * number,
        in_specs=[pl.BlockSpec(memory_space=pltpu.HBM)] * (1 + number),
        out_specs=[whole_vmem] * (2 + number),
        scratch_shapes=[pltpu.VMEM(f.shape, jnp.float32) for f in fields[:number]]
        + [pltpu.VMEM((2, lag_count, ROWS, width), jnp.float32), pltpu.SemaphoreType.DMA((2 + number,))],
        compiler_params=pltpu.CompilerParams(vmem_limit_bytes=SUM_BYTES),
        name="send_rows",
    )(*(in_hbm(a) for a in (image_grad, *fields[:number])))
    near = strip_swap(near, 1)
    following = lax.ppermute(
        following, "strip", [p for i in range(1, count, 2) for p in ((i, (i + 1) % count), ((i + 1) % count, i))]
    )
    if not direct:
        whole = []
        for field in fields:
            cut = field.reshape(snaps, count, depth, columns).transpose(1, 3, 0, 2)
            cut = lax.all_to_all(cut.reshape(count, columns, snaps * depth), "strip", 0, 0, tiled=True)
            whole.append([cut.reshape(count * columns, snaps * depth)])
        return near, following, whole, [None] * len(fields)

    everything = tuple(range(number))
    sends = [(at, everything) for at in range(1, pieces - ALONE)]
    sends += [(at, (f,)) for f in everything for at in range(pieces - ALONE, pieces)]
    out_shape = [buffer(2 * len(group) * LANES) for _, group in sends]
    packed = pl.pallas_call(
        functools.partial(pack_kernel, pieces, edge_rows, sends),
        out_shape=out_shape,
        in_specs=[whole_vmem] * (number + 1),
        out_specs=[whole_vmem] * len(out_shape),
        compiler_params=pltpu.CompilerParams(vmem_limit_bytes=SMALL_BYTES),
        name="pack_fields",
    )(*mine, near)
    sent = [strip_swap(part, 2 * at) for (at, _), part in zip(sends, packed)]
    whole, where_at = [], []
    for f in range(number):
        came = [(at, group.index(f), part) for (at, group), part in zip(sends, sent) if f in group]
        whole.append([mine[f], near] + [part for _, _, part in came])
        where_at.append([(0, 0, 0), (1, edge_rows + f * pieces * LANES, 1)])
        for index, (at, place, _) in enumerate(came):
            for side in range(2):
                where_at[f].append((2 + index, (2 * place + side) * LANES, 2 * at + side))
    return near, following, whole, where_at


def exchange(parts, distance):
    count = lax.axis_size("lag")
    return lax.ppermute(parts, "lag", [(i, i ^ distance) for i in range(count)])


def turn_back_kernel(*refs):
    out_ref = refs[-1]
    snaps, depth, width = out_ref.shape
    for at in range(width // LANES):
        rows = pl.ds(at * LANES, LANES)
        total = refs[0][rows]
        for ref in refs[1:-1]:
            total = total + ref[rows]
        turned = total.T
        for snap in range(snaps):
            out_ref[snap, :, rows] = turned[snap * depth : (snap + 1) * depth]


def lag_send(part, *pairs):
    return lax.ppermute(part, "lag", pairs)


def sum_places(form, parts, snaps):
    if form == "direct":
        terms = [parts[0]] + [exchange(part, d) for d, part in enumerate(parts) if d]
    elif form == "halves":
        keep, send = parts
        came = exchange(send, 1)
        rows = keep.shape[0] // 2
        terms = [keep[:rows], came[:rows], exchange(keep[rows:] + came[rows:], 3)]
    else:
        keep, second, both, mirror = parts
        rows = keep.shape[0]
        came = exchange(both, 1)
        skip = lag_send(second, (0, 2), (3, 1))
        middle = lag_send(mirror, (1, 2), (2, 1))
        passed = lag_send(second + came[:rows], (1, 3), (2, 0))
        terms = [keep, came[rows:], skip, middle, passed]
    rows, lanes = terms[-1].shape
    return pl.pallas_call(
        turn_back_kernel,
        out_shape=jax.ShapeDtypeStruct((snaps, lanes // snaps, rows), jnp.float32),
        in_specs=[whole_vmem] * len(terms),
        out_specs=whole_vmem,
        compiler_params=pltpu.CompilerParams(vmem_limit_bytes=SMALL_BYTES),
        name="turn_back",
    )(*terms)


def local(image_grad, source_field, receiver_field):
    lag_count, depth, width = image_grad.shape
    snaps = source_field.shape[0]
    pad = lax.axis_size("lag") * lag_count // 2
    near, following, (receiver, source), (at_first, at_second) = gather_rows(
        image_grad, [receiver_field, source_field]
    )
    slabs = filter_slabs(image_grad, near, following, pad)
    first = sum_lags(1, FIRST_FORM, slabs, receiver, at_first, width)
    second = sum_lags(-1, SECOND_FORM, slabs, source, at_second, width, first[:1] if ORDERED else ())
    return sum_places(FIRST_FORM, first, snaps), sum_places(SECOND_FORM, second, snaps)


def solution(mesh):
    in_specs = (P("lag", "strip", None), P(None, None, "strip"), P(None, None, "strip"))
    out_specs = (P(None, "strip", "lag"), P(None, "strip", "lag"))
    return jax.shard_map(local, mesh=mesh, in_specs=in_specs, out_specs=out_specs, check_vma=False)
```

```python
import functools

import jax
import jax.numpy as jnp
from jax import lax
from jax.experimental import pallas as pl
from jax.experimental.pallas import tpu as pltpu
from jax.sharding import PartitionSpec as P

LANES = 128
ROWS = 8
CLASSES = 4
PAIRS = 4
CHUNK = 512
ALONE = 1
FIRST_FORM = "halves"
SECOND_FORM = "direct"
ORDERED = True
GRAD_IN_HBM = True
FILTER_COST = 3 * 10**9
FIRST_COST = 0
SECOND_COST = 10**9
BACK_COST = 5 * 10**10
CHAIN = True
FILTER_BYTES = 32 * 1024 * 1024
SUM_BYTES = 8 * 1024 * 1024
SMALL_BYTES = 4 * 1024 * 1024

def weight(size):
    return pl.CostEstimate(flops=size, bytes_accessed=min(size, 10**7), transcendentals=0)


def in_hbm(array):
    return pltpu.with_memory_space_constraint(array, pltpu.HBM)


whole_vmem = pl.BlockSpec(memory_space=pltpu.VMEM)


def filter_kernel(pad, grad_hbm, near_ref, next_ref, out_ref, edge_parts, held, sems, *turned):
    lag_count, depth, width = grad_hbm.shape
    half = lag_count // 2
    tiles = width // LANES
    steps = half // PAIRS

    def fetch(step, side):
        lags = pl.ds(step * PAIRS + side * half, PAIRS)
        return pltpu.make_async_copy(grad_hbm.at[lags], held.at[lags], sems.at[2 * step + side])

    for step in range(steps):
        for side in range(2):
            fetch(step, side).start()

    centers = turned
    strip = lax.axis_index("strip")
    core = lax.rem(strip, 2)
    inside = (strip != 0) & (strip != lax.axis_size("strip") - 1)
    blank = jnp.zeros((LANES - 2 * lag_count, LANES), jnp.float32)

    def split(value):
        high = value.astype(jnp.bfloat16)
        return high, (value - high.astype(jnp.float32)).astype(jnp.bfloat16)

    for t in range(tiles):
        rows = pl.ds(t * lag_count, lag_count)
        near, following = near_ref[rows], jnp.where(inside, next_ref[rows], 0.0)
        above = jnp.where(core == 0, following, near)
        below = jnp.where(core == 0, near, following)
        parts = split(jnp.concatenate([above, below, blank], 0).T)
        for part in range(2):
            edge_parts[part, pl.ds(t * LANES, LANES)] = parts[part]
    out_ref[:, pl.ds(0, pad)] = jnp.zeros((half, pad, LANES), jnp.float32)
    out_ref[:, pl.ds(pad + width, pad)] = jnp.zeros((half, pad, LANES), jnp.float32)
    for center_t in centers:
        center_t[pl.ds(0, ROWS)] = jnp.zeros((ROWS, LANES), jnp.float32)
        center_t[pl.ds(ROWS + width, ROWS)] = jnp.zeros((ROWS, LANES), jnp.float32)

    def body(step, carry):
        fetch(step, 0).wait()
        fetch(step, 1).wait()
        low_ref, high_ref = held.at[pl.ds(step * PAIRS, PAIRS)], held.at[pl.ds(step * PAIRS + half, PAIRS)]
        source = lax.broadcasted_iota(jnp.int32, (LANES, LANES), 0)
        target = lax.broadcasted_iota(jnp.int32, (LANES, LANES), 1)
        beside = (jnp.abs(source - target) == 1) & ((source < depth) == (target < depth))
        band = jnp.where(source == target, 2.0, jnp.where(beside, -0.25, 0.0))
        upper = jnp.where(target == 0, 0, jnp.where(target == depth, half, 2 * LANES))
        lower = jnp.where(target == depth - 1, 0, jnp.where(target == 2 * depth - 1, half, 2 * LANES))
        matrices = []
        for within in range(PAIRS):
            lag = step * PAIRS + within
            chosen = (source == upper + lag) | (source == lower + lag + lag_count)
            choice = jnp.where(chosen, -0.25, 0.0)
            matrices.append(jnp.concatenate([band, choice], 0).astype(jnp.bfloat16))

        def turn(within, t):
            rows = pl.ds(t * LANES, LANES)
            center = jnp.concatenate([low_ref[within, :, rows], high_ref[within, :, rows]], 0).T
            centers[within][pl.ds(ROWS + t * LANES, LANES)] = center

        def join(within, at):
            rows = pl.ds(at * chunk, chunk)
            west = centers[within][pl.ds(ROWS - 1 + at * chunk, chunk)]
            east = centers[within][pl.ds(ROWS + 1 + at * chunk, chunk)]
            parts = split(centers[within][pl.ds(ROWS + at * chunk, chunk)])
            products = [
                jnp.dot(
                    jnp.concatenate([parts[part], edge_parts[part, rows]], 1),
                    matrices[within],
                    preferred_element_type=jnp.float32,
                )
                for part in range(2)
            ]
            value = (products[0] + products[1]) - 0.25 * (west + east)
            out_ref[step * PAIRS + within, pl.ds(pad + at * chunk, chunk)] = value

        chunk = min(CHUNK, width)
        for within in range(PAIRS + 1):
            for t in range(tiles):
                if within < PAIRS:
                    turn(within, t)
                if within and (t + 1) * LANES % chunk == 0:
                    join(within - 1, ((t + 1) * LANES // chunk) - 1)
        return carry

    lax.fori_loop(0, steps, body, 0)


def filter_slabs(image_grad, from_near, from_next, pad):
    lag_count, depth, width = image_grad.shape
    return pl.pallas_call(
        functools.partial(filter_kernel, pad),
        out_shape=jax.ShapeDtypeStruct((lag_count // 2, width + 2 * pad, 2 * depth), jnp.float32),
        in_specs=[pl.BlockSpec(memory_space=pltpu.HBM if GRAD_IN_HBM else pl.ANY), whole_vmem, whole_vmem],
        out_specs=whole_vmem,
        scratch_shapes=[pltpu.VMEM((2, width, LANES), jnp.bfloat16)]
        + [pltpu.VMEM(image_grad.shape, jnp.float32), pltpu.SemaphoreType.DMA((lag_count // PAIRS,))]
        + [pltpu.VMEM((width + 2 * ROWS, LANES), jnp.float32)] * PAIRS,
        compiler_params=pltpu.CompilerParams(vmem_limit_bytes=FILTER_BYTES),
        cost_estimate=weight(FILTER_COST),
        name="filter_slabs",
    )(in_hbm(image_grad) if GRAD_IN_HBM else image_grad, from_near, from_next)


def sum_kernel(sign, places, where_at, blocks, slab_ref, *refs):
    number = len(blocks)
    pieces, outs = refs[: -3 - number], refs[-3 - number : -3]
    field_ref, paired, acc = refs[-3:]
    half, slab_rows, _ = slab_ref.shape
    width = field_ref.shape[0]
    if where_at is None:
        field_ref[...] = pieces[0][...]
    else:
        strip = lax.axis_index("strip")
        for index, row, distance in where_at:
            rows = pl.multiple_of((strip ^ distance) * LANES, LANES)
            field_ref[pl.ds(rows, LANES)] = pieces[index][pl.ds(row, LANES)]
    pad = (slab_rows - width) // 2
    lag_count = 2 * half
    margin = 2 * pad + 2 * half
    place = lax.axis_index("lag")
    first = place * lag_count - pad
    spread = width + half
    block_rows = ROWS * max(m for m in range(1, 11) if spread // ROWS % m == 0)
    low_at = 0 if sign > 0 else half
    high_at = half - low_at

    for snap in range(2):
        blank = jnp.zeros((margin + half, LANES), jnp.float32)
        paired[snap, pl.ds(0, margin)] = blank[:margin]
        paired[snap, pl.ds(margin + width, margin)] = blank[:margin]
    low = lax.broadcasted_iota(jnp.int32, (LANES, LANES), 1) < LANES // 2
    edge = jnp.zeros((half, LANES), jnp.float32)
    field = field_ref[...]
    lower = lax.broadcasted_iota(jnp.int32, (spread, LANES), 1) < LANES // 2
    if sign > 0:
        here = jnp.concatenate([edge, field], 0)
        there = jnp.concatenate([field, edge], 0)
        start = margin - half
    else:
        here = jnp.concatenate([field, edge], 0)
        there = jnp.concatenate([edge, field], 0)
        start = margin
    paired[0, pl.ds(start, spread)] = jnp.where(lower, here, pltpu.roll(there, LANES // 2, 1))
    paired[1, pl.ds(start, spread)] = jnp.where(lower, pltpu.roll(here, LANES // 2, 1), there)

    tall = block_rows // ROWS
    per_class = half // CLASSES

    def block(at, carry):
        y = at * block_rows - low_at
        slab_at = pl.multiple_of(pad + y + sign * first, ROWS)
        field_at = pl.multiple_of(margin + y + sign * 2 * first, ROWS)
        totals = [[None] * tall for _ in range(2)]
        for cls in range(CLASSES):
            held = {}
            for step in range(per_class):
                lag = step * CLASSES + cls
                for up in range(tall):
                    slab = slab_ref[lag, pl.ds(slab_at + sign * lag + up * ROWS, ROWS)]
                    for snap in range(2):
                        row = sign * 2 * lag + up * ROWS
                        if (snap, row) not in held:
                            held[snap, row] = paired[snap, pl.ds(field_at + row, ROWS)]
                        term = slab * held[snap, row]
                        total = totals[snap][up]
                        totals[snap][up] = term if total is None else total + term
        for snap in range(2):
            for up in range(tall):
                rows = pl.multiple_of(at * block_rows + up * ROWS, ROWS)
                acc[snap, pl.ds(rows, ROWS)] = totals[snap][up]
        return carry

    lax.fori_loop(0, spread // block_rows, block, 0)

    part = width // places

    def finish(target, slot, source):
        for piece in range(part // LANES):
            x = pl.multiple_of(source * part + piece * LANES, LANES)
            at_low = pl.ds(x + low_at, LANES)
            at_high = pl.ds(x + high_at, LANES)
            straight = jnp.where(low, acc[0, at_low], acc[1, at_high])
            crossed = jnp.where(low, acc[1, at_low], acc[0, at_high])
            rows = pl.ds(slot * part + piece * LANES, LANES)
            target[rows] = straight + pltpu.roll(crossed, LANES // 2, 1)

    for target, distances in zip(outs, blocks):
        for slot, distance in enumerate(distances):
            finish(target, slot, place ^ distance)


BLOCKS = {
    "direct": ((0,), (1,), (2,), (3,)),
    "halves": ((0, 3), (1, 2)),
    "forward": ((0,), (2,), (3, 1), (3,)),
}


def sum_lags(sign, form, slabs, pieces, where_at, width, after=()):
    half, slab_rows, _ = slabs.shape
    pad = (slab_rows - width) // 2
    margin = 2 * pad + 2 * half
    places = lax.axis_size("lag")
    part = width // places
    out_shape = [jax.ShapeDtypeStruct((len(held) * part, LANES), jnp.float32) for held in BLOCKS[form]]
    return pl.pallas_call(
        functools.partial(sum_kernel, sign, places, where_at, BLOCKS[form]),
        out_shape=out_shape,
        in_specs=[whole_vmem] * (1 + len(pieces) + len(after)),
        out_specs=[whole_vmem] * len(out_shape),
        scratch_shapes=[
            pltpu.VMEM((width, LANES), jnp.float32),
            pltpu.VMEM((2, width + 2 * margin, LANES), jnp.float32),
            pltpu.VMEM((2, width + half, LANES), jnp.float32),
        ],
        compiler_params=pltpu.CompilerParams(vmem_limit_bytes=SUM_BYTES),
        cost_estimate=weight(FIRST_COST if sign > 0 else SECOND_COST),
        name="sum_lags",
    )(slabs, *pieces, *after)


def send_kernel(pieces, grad_hbm, *refs):
    lag_count, depth, width = grad_hbm.shape
    tiles = width // LANES
    number = (len(refs) - 4) // 3
    fields, near_ref, next_ref = refs[:number], refs[number], refs[number + 1]
    mine = refs[number + 2 : 2 * number + 2]
    held, edges, sems = refs[2 * number + 2 : 3 * number + 2], refs[-2], refs[-1]
    strip = lax.axis_index("strip")
    core = lax.rem(strip, 2)
    copies = []
    for side in range(2):
        rows = pl.ds(side * (depth - ROWS), ROWS)
        copies.append(pltpu.make_async_copy(grad_hbm.at[:, rows], edges.at[side], sems.at[side]))
    for f in range(number):
        copies.append(pltpu.make_async_copy(fields[f], held[f], sems.at[2 + f]))
    for copy in copies[2:] + copies[:2]:
        copy.start()

    for f in range(number):
        copies[2 + f].wait()
        snaps = held[f].shape[0]
        for at in range(pieces):
            for side in range(2):
                first = pl.multiple_of((strip ^ (2 * at + side)) * depth, depth)
                rows = [held[f][s, pl.ds(first, depth)] for s in range(snaps)]
                piece = jnp.concatenate(rows, 0).T
                if side:
                    start = lag_count * tiles + (f * pieces + at) * LANES
                    near_ref[pl.ds(start, LANES)] = piece
                else:
                    mine[f][pl.ds(at * LANES, LANES)] = piece

    copies[0].wait()
    copies[1].wait()
    low = core == 0
    for t in range(tiles):
        lanes = pl.ds(t * LANES, LANES)
        top = edges[0, :, 0, lanes]
        bottom = edges[1, :, ROWS - 1, lanes]
        rows = pl.ds(t * lag_count, lag_count)
        near_ref[rows] = jnp.where(low, bottom, top)
        next_ref[rows] = jnp.where(low, top, bottom)


def pack_kernel(pieces, edge_rows, sends, *refs):
    number = 1 + max(f for _, group in sends for f in group)
    mine, near_ref, out = refs[:number], refs[number], refs[number + 1 :]
    for (at, group), out_ref in zip(sends, out):
        for place, f in enumerate(group):
            rows = pl.ds(at * LANES, LANES)
            out_ref[pl.ds(2 * place * LANES, LANES)] = mine[f][rows]
            far = pl.ds(edge_rows + (f * pieces + at) * LANES, LANES)
            out_ref[pl.ds((2 * place + 1) * LANES, LANES)] = near_ref[far]


def strip_swap(part, distance):
    count = lax.axis_size("strip")
    return lax.ppermute(part, "strip", [(i, i ^ distance) for i in range(count)])


def gather_rows(image_grad, fields):
    lag_count, depth, width = image_grad.shape
    count = lax.axis_size("strip")
    snaps, all_rows, columns = fields[0].shape
    direct = columns == LANES and count >= 4 and count & (count - 1) == 0
    pieces = count // 2 if direct else 0
    number = len(fields) if direct else 0
    edge_rows = lag_count * (width // LANES)

    def buffer(rows):
        return jax.ShapeDtypeStruct((rows, LANES), jnp.float32)

    near, following, *mine = pl.pallas_call(
        functools.partial(send_kernel, pieces),
        out_shape=[buffer(edge_rows + number * pieces * LANES), buffer(edge_rows)]
        + [buffer(pieces * LANES)] * number,
        in_specs=[pl.BlockSpec(memory_space=pltpu.HBM)] * (1 + number),
        out_specs=[whole_vmem] * (2 + number),
        scratch_shapes=[pltpu.VMEM(f.shape, jnp.float32) for f in fields[:number]]
        + [pltpu.VMEM((2, lag_count, ROWS, width), jnp.float32), pltpu.SemaphoreType.DMA((2 + number,))],
        compiler_params=pltpu.CompilerParams(vmem_limit_bytes=SUM_BYTES),
        name="send_rows",
    )(*(in_hbm(a) for a in (image_grad, *fields[:number])))
    near = strip_swap(near, 1)
    following = lax.ppermute(
        following, "strip", [p for i in range(1, count, 2) for p in ((i, (i + 1) % count), ((i + 1) % count, i))]
    )
    if not direct:
        whole = []
        for field in fields:
            cut = field.reshape(snaps, count, depth, columns).transpose(1, 3, 0, 2)
            cut = lax.all_to_all(cut.reshape(count, columns, snaps * depth), "strip", 0, 0, tiled=True)
            whole.append([cut.reshape(count * columns, snaps * depth)])
        return near, following, whole, [None] * len(fields)

    everything = tuple(range(number))
    sends = [(at, everything) for at in range(1, pieces - ALONE)]
    sends += [(at, (f,)) for f in everything for at in range(pieces - ALONE, pieces)]
    out_shape = [buffer(2 * len(group) * LANES) for _, group in sends]
    packed = pl.pallas_call(
        functools.partial(pack_kernel, pieces, edge_rows, sends),
        out_shape=out_shape,
        in_specs=[whole_vmem] * (number + 1),
        out_specs=[whole_vmem] * len(out_shape),
        compiler_params=pltpu.CompilerParams(vmem_limit_bytes=SMALL_BYTES),
        name="pack_fields",
    )(*mine, near)
    sent = [strip_swap(part, 2 * at) for (at, _), part in zip(sends, packed)]
    whole, where_at = [], []
    for f in range(number):
        came = [(at, group.index(f), part) for (at, group), part in zip(sends, sent) if f in group]
        whole.append([mine[f], near] + [part for _, _, part in came])
        where_at.append([(0, 0, 0), (1, edge_rows + f * pieces * LANES, 1)])
        for index, (at, place, _) in enumerate(came):
            for side in range(2):
                where_at[f].append((2 + index, (2 * place + side) * LANES, 2 * at + side))
    return near, following, whole, where_at


def exchange(parts, distance):
    count = lax.axis_size("lag")
    return lax.ppermute(parts, "lag", [(i, i ^ distance) for i in range(count)])


def turn_back_kernel(*refs):
    out_ref = refs[-1]
    snaps, depth, width = out_ref.shape
    for at in range(width // LANES):
        rows = pl.ds(at * LANES, LANES)
        total = refs[0][rows]
        for ref in refs[1:-1]:
            total = total + ref[rows]
        turned = total.T
        for snap in range(snaps):
            out_ref[snap, :, rows] = turned[snap * depth : (snap + 1) * depth]


def add_kernel(keep_ref, came_ref, *refs):
    rows = refs[-1].shape[0]
    refs[-1][...] = keep_ref[pl.ds(rows, rows)] + came_ref[pl.ds(rows, rows)]


def lag_send(part, *pairs):
    return lax.ppermute(part, "lag", pairs)


def sum_places(form, parts, snaps, after=()):
    if form == "direct":
        terms = [parts[0]] + [exchange(part, d) for d, part in enumerate(parts) if d]
    elif form == "halves":
        keep, send = parts
        came = exchange(send, 1)
        rows = keep.shape[0] // 2
        passed = pl.pallas_call(
            add_kernel,
            out_shape=jax.ShapeDtypeStruct((rows, keep.shape[1]), jnp.float32),
            in_specs=[whole_vmem] * 2 + [pl.BlockSpec(memory_space=pltpu.HBM)] * len(after),
            out_specs=whole_vmem,
            compiler_params=pltpu.CompilerParams(vmem_limit_bytes=SMALL_BYTES),
            name="add_mirror",
        )(keep, came, *(in_hbm(a) for a in after))
        terms = [keep, came, exchange(passed, 3)]
    else:
        keep, second, both, mirror = parts
        rows = keep.shape[0]
        came = exchange(both, 1)
        skip = lag_send(second, (0, 2), (3, 1))
        middle = lag_send(mirror, (1, 2), (2, 1))
        passed = lag_send(second + came[:rows], (1, 3), (2, 0))
        terms = [keep, came[rows:], skip, middle, passed]
    rows, lanes = terms[-1].shape
    return pl.pallas_call(
        turn_back_kernel,
        out_shape=jax.ShapeDtypeStruct((snaps, lanes // snaps, rows), jnp.float32),
        in_specs=[whole_vmem] * len(terms),
        out_specs=whole_vmem,
        compiler_params=pltpu.CompilerParams(vmem_limit_bytes=SMALL_BYTES),
        cost_estimate=weight(BACK_COST),
        name="turn_back",
    )(*terms)


def local(image_grad, source_field, receiver_field):
    lag_count, depth, width = image_grad.shape
    snaps = source_field.shape[0]
    pad = lax.axis_size("lag") * lag_count // 2
    near, following, (receiver, source), (at_first, at_second) = gather_rows(
        image_grad, [receiver_field, source_field]
    )
    slabs = filter_slabs(image_grad, near, following, pad)
    first = sum_lags(1, FIRST_FORM, slabs, receiver, at_first, width)
    second = sum_lags(-1, SECOND_FORM, slabs, source, at_second, width, first[:1] if ORDERED else ())
    source_adjoint = sum_places(FIRST_FORM, first, snaps)
    receiver_adjoint = sum_places(SECOND_FORM, second, snaps, (source_adjoint,) if CHAIN else ())
    return source_adjoint, receiver_adjoint


def solution(mesh):
    in_specs = (P("lag", "strip", None), P(None, None, "strip"), P(None, None, "strip"))
    out_specs = (P(None, "strip", "lag"), P(None, "strip", "lag"))
    return jax.shard_map(local, mesh=mesh, in_specs=in_specs, out_specs=out_specs, check_vma=False)
```

```python
import functools

import jax
import jax.numpy as jnp
from jax import lax
from jax.experimental import pallas as pl
from jax.experimental.pallas import tpu as pltpu
from jax.sharding import PartitionSpec as P

LANES = 128
ROWS = 8
CLASSES = 4
PAIRS = 4
CHUNK = 512
ALONE = 1
FIRST_FORM = "halves"
SECOND_FORM = "direct"
ORDERED = True
GRAD_IN_HBM = True
FILTER_COST = 3 * 10**9
FIRST_COST = 0
SECOND_COST = 10**9
BACK_COST = 5 * 10**10
CHAIN = True
DIRECT_ORDER = (2, 3, 1)
FILTER_BYTES = 32 * 1024 * 1024
SUM_BYTES = 8 * 1024 * 1024
SMALL_BYTES = 4 * 1024 * 1024

def weight(size):
    return pl.CostEstimate(flops=size, bytes_accessed=min(size, 10**7), transcendentals=0)


def in_hbm(array):
    return pltpu.with_memory_space_constraint(array, pltpu.HBM)


whole_vmem = pl.BlockSpec(memory_space=pltpu.VMEM)


def filter_kernel(pad, grad_hbm, near_ref, next_ref, out_ref, edge_parts, held, sems, *turned):
    lag_count, depth, width = grad_hbm.shape
    half = lag_count // 2
    tiles = width // LANES
    steps = half // PAIRS

    def fetch(step, side):
        lags = pl.ds(step * PAIRS + side * half, PAIRS)
        return pltpu.make_async_copy(grad_hbm.at[lags], held.at[lags], sems.at[2 * step + side])

    for step in range(steps):
        for side in range(2):
            fetch(step, side).start()

    centers = turned
    strip = lax.axis_index("strip")
    core = lax.rem(strip, 2)
    inside = (strip != 0) & (strip != lax.axis_size("strip") - 1)
    blank = jnp.zeros((LANES - 2 * lag_count, LANES), jnp.float32)

    def split(value):
        high = value.astype(jnp.bfloat16)
        return high, (value - high.astype(jnp.float32)).astype(jnp.bfloat16)

    for t in range(tiles):
        rows = pl.ds(t * lag_count, lag_count)
        near, following = near_ref[rows], jnp.where(inside, next_ref[rows], 0.0)
        above = jnp.where(core == 0, following, near)
        below = jnp.where(core == 0, near, following)
        parts = split(jnp.concatenate([above, below, blank], 0).T)
        for part in range(2):
            edge_parts[part, pl.ds(t * LANES, LANES)] = parts[part]
    out_ref[:, pl.ds(0, pad)] = jnp.zeros((half, pad, LANES), jnp.float32)
    out_ref[:, pl.ds(pad + width, pad)] = jnp.zeros((half, pad, LANES), jnp.float32)
    for center_t in centers:
        center_t[pl.ds(0, ROWS)] = jnp.zeros((ROWS, LANES), jnp.float32)
        center_t[pl.ds(ROWS + width, ROWS)] = jnp.zeros((ROWS, LANES), jnp.float32)

    def body(step, carry):
        fetch(step, 0).wait()
        fetch(step, 1).wait()
        low_ref, high_ref = held.at[pl.ds(step * PAIRS, PAIRS)], held.at[pl.ds(step * PAIRS + half, PAIRS)]
        source = lax.broadcasted_iota(jnp.int32, (LANES, LANES), 0)
        target = lax.broadcasted_iota(jnp.int32, (LANES, LANES), 1)
        beside = (jnp.abs(source - target) == 1) & ((source < depth) == (target < depth))
        band = jnp.where(source == target, 2.0, jnp.where(beside, -0.25, 0.0))
        upper = jnp.where(target == 0, 0, jnp.where(target == depth, half, 2 * LANES))
        lower = jnp.where(target == depth - 1, 0, jnp.where(target == 2 * depth - 1, half, 2 * LANES))
        matrices = []
        for within in range(PAIRS):
            lag = step * PAIRS + within
            chosen = (source == upper + lag) | (source == lower + lag + lag_count)
            choice = jnp.where(chosen, -0.25, 0.0)
            matrices.append(jnp.concatenate([band, choice], 0).astype(jnp.bfloat16))

        def turn(within, t):
            rows = pl.ds(t * LANES, LANES)
            center = jnp.concatenate([low_ref[within, :, rows], high_ref[within, :, rows]], 0).T
            centers[within][pl.ds(ROWS + t * LANES, LANES)] = center

        def join(within, at):
            rows = pl.ds(at * chunk, chunk)
            west = centers[within][pl.ds(ROWS - 1 + at * chunk, chunk)]
            east = centers[within][pl.ds(ROWS + 1 + at * chunk, chunk)]
            parts = split(centers[within][pl.ds(ROWS + at * chunk, chunk)])
            products = [
                jnp.dot(
                    jnp.concatenate([parts[part], edge_parts[part, rows]], 1),
                    matrices[within],
                    preferred_element_type=jnp.float32,
                )
                for part in range(2)
            ]
            value = (products[0] + products[1]) - 0.25 * (west + east)
            out_ref[step * PAIRS + within, pl.ds(pad + at * chunk, chunk)] = value

        chunk = min(CHUNK, width)
        for within in range(PAIRS + 1):
            for t in range(tiles):
                if within < PAIRS:
                    turn(within, t)
                if within and (t + 1) * LANES % chunk == 0:
                    join(within - 1, ((t + 1) * LANES // chunk) - 1)
        return carry

    lax.fori_loop(0, steps, body, 0)


def filter_slabs(image_grad, from_near, from_next, pad):
    lag_count, depth, width = image_grad.shape
    return pl.pallas_call(
        functools.partial(filter_kernel, pad),
        out_shape=jax.ShapeDtypeStruct((lag_count // 2, width + 2 * pad, 2 * depth), jnp.float32),
        in_specs=[pl.BlockSpec(memory_space=pltpu.HBM if GRAD_IN_HBM else pl.ANY), whole_vmem, whole_vmem],
        out_specs=whole_vmem,
        scratch_shapes=[pltpu.VMEM((2, width, LANES), jnp.bfloat16)]
        + [pltpu.VMEM(image_grad.shape, jnp.float32), pltpu.SemaphoreType.DMA((lag_count // PAIRS,))]
        + [pltpu.VMEM((width + 2 * ROWS, LANES), jnp.float32)] * PAIRS,
        compiler_params=pltpu.CompilerParams(vmem_limit_bytes=FILTER_BYTES),
        cost_estimate=weight(FILTER_COST),
        name="filter_slabs",
    )(in_hbm(image_grad) if GRAD_IN_HBM else image_grad, from_near, from_next)


def sum_kernel(sign, places, where_at, blocks, slab_ref, *refs):
    number = len(blocks)
    pieces, outs = refs[: -3 - number], refs[-3 - number : -3]
    field_ref, paired, acc = refs[-3:]
    half, slab_rows, _ = slab_ref.shape
    width = field_ref.shape[0]
    if where_at is None:
        field_ref[...] = pieces[0][...]
    else:
        strip = lax.axis_index("strip")
        for index, row, distance in where_at:
            rows = pl.multiple_of((strip ^ distance) * LANES, LANES)
            field_ref[pl.ds(rows, LANES)] = pieces[index][pl.ds(row, LANES)]
    pad = (slab_rows - width) // 2
    lag_count = 2 * half
    margin = 2 * pad + 2 * half
    place = lax.axis_index("lag")
    first = place * lag_count - pad
    spread = width + half
    block_rows = ROWS * max(m for m in range(1, 11) if spread // ROWS % m == 0)
    low_at = 0 if sign > 0 else half
    high_at = half - low_at

    for snap in range(2):
        blank = jnp.zeros((margin + half, LANES), jnp.float32)
        paired[snap, pl.ds(0, margin)] = blank[:margin]
        paired[snap, pl.ds(margin + width, margin)] = blank[:margin]
    low = lax.broadcasted_iota(jnp.int32, (LANES, LANES), 1) < LANES // 2
    edge = jnp.zeros((half, LANES), jnp.float32)
    field = field_ref[...]
    lower = lax.broadcasted_iota(jnp.int32, (spread, LANES), 1) < LANES // 2
    if sign > 0:
        here = jnp.concatenate([edge, field], 0)
        there = jnp.concatenate([field, edge], 0)
        start = margin - half
    else:
        here = jnp.concatenate([field, edge], 0)
        there = jnp.concatenate([edge, field], 0)
        start = margin
    paired[0, pl.ds(start, spread)] = jnp.where(lower, here, pltpu.roll(there, LANES // 2, 1))
    paired[1, pl.ds(start, spread)] = jnp.where(lower, pltpu.roll(here, LANES // 2, 1), there)

    tall = block_rows // ROWS
    per_class = half // CLASSES

    def block(at, carry):
        y = at * block_rows - low_at
        slab_at = pl.multiple_of(pad + y + sign * first, ROWS)
        field_at = pl.multiple_of(margin + y + sign * 2 * first, ROWS)
        totals = [[None] * tall for _ in range(2)]
        for cls in range(CLASSES):
            held = {}
            for step in range(per_class):
                lag = step * CLASSES + cls
                for up in range(tall):
                    slab = slab_ref[lag, pl.ds(slab_at + sign * lag + up * ROWS, ROWS)]
                    for snap in range(2):
                        row = sign * 2 * lag + up * ROWS
                        if (snap, row) not in held:
                            held[snap, row] = paired[snap, pl.ds(field_at + row, ROWS)]
                        term = slab * held[snap, row]
                        total = totals[snap][up]
                        totals[snap][up] = term if total is None else total + term
        for snap in range(2):
            for up in range(tall):
                rows = pl.multiple_of(at * block_rows + up * ROWS, ROWS)
                acc[snap, pl.ds(rows, ROWS)] = totals[snap][up]
        return carry

    lax.fori_loop(0, spread // block_rows, block, 0)

    part = width // places

    def finish(target, slot, source):
        for piece in range(part // LANES):
            x = pl.multiple_of(source * part + piece * LANES, LANES)
            at_low = pl.ds(x + low_at, LANES)
            at_high = pl.ds(x + high_at, LANES)
            straight = jnp.where(low, acc[0, at_low], acc[1, at_high])
            crossed = jnp.where(low, acc[1, at_low], acc[0, at_high])
            rows = pl.ds(slot * part + piece * LANES, LANES)
            target[rows] = straight + pltpu.roll(crossed, LANES // 2, 1)

    for target, distances in zip(outs, blocks):
        for slot, distance in enumerate(distances):
            finish(target, slot, place ^ distance)


BLOCKS = {
    "direct": ((0,), (1,), (2,), (3,)),
    "halves": ((0, 3), (1, 2)),
    "forward": ((0,), (2,), (3, 1), (3,)),
}


def sum_lags(sign, form, slabs, pieces, where_at, width, after=()):
    half, slab_rows, _ = slabs.shape
    pad = (slab_rows - width) // 2
    margin = 2 * pad + 2 * half
    places = lax.axis_size("lag")
    part = width // places
    out_shape = [jax.ShapeDtypeStruct((len(held) * part, LANES), jnp.float32) for held in BLOCKS[form]]
    return pl.pallas_call(
        functools.partial(sum_kernel, sign, places, where_at, BLOCKS[form]),
        out_shape=out_shape,
        in_specs=[whole_vmem] * (1 + len(pieces) + len(after)),
        out_specs=[whole_vmem] * len(out_shape),
        scratch_shapes=[
            pltpu.VMEM((width, LANES), jnp.float32),
            pltpu.VMEM((2, width + 2 * margin, LANES), jnp.float32),
            pltpu.VMEM((2, width + half, LANES), jnp.float32),
        ],
        compiler_params=pltpu.CompilerParams(vmem_limit_bytes=SUM_BYTES),
        cost_estimate=weight(FIRST_COST if sign > 0 else SECOND_COST),
        name="sum_lags",
    )(slabs, *pieces, *after)


def send_kernel(pieces, grad_hbm, *refs):
    lag_count, depth, width = grad_hbm.shape
    tiles = width // LANES
    number = (len(refs) - 4) // 3
    fields, near_ref, next_ref = refs[:number], refs[number], refs[number + 1]
    mine = refs[number + 2 : 2 * number + 2]
    held, edges, sems = refs[2 * number + 2 : 3 * number + 2], refs[-2], refs[-1]
    strip = lax.axis_index("strip")
    core = lax.rem(strip, 2)
    copies = []
    for side in range(2):
        rows = pl.ds(side * (depth - ROWS), ROWS)
        copies.append(pltpu.make_async_copy(grad_hbm.at[:, rows], edges.at[side], sems.at[side]))
    for f in range(number):
        copies.append(pltpu.make_async_copy(fields[f], held[f], sems.at[2 + f]))
    for copy in copies[2:] + copies[:2]:
        copy.start()

    for f in range(number):
        copies[2 + f].wait()
        snaps = held[f].shape[0]
        for at in range(pieces):
            for side in range(2):
                first = pl.multiple_of((strip ^ (2 * at + side)) * depth, depth)
                rows = [held[f][s, pl.ds(first, depth)] for s in range(snaps)]
                piece = jnp.concatenate(rows, 0).T
                if side:
                    start = lag_count * tiles + (f * pieces + at) * LANES
                    near_ref[pl.ds(start, LANES)] = piece
                else:
                    mine[f][pl.ds(at * LANES, LANES)] = piece

    copies[0].wait()
    copies[1].wait()
    low = core == 0
    for t in range(tiles):
        lanes = pl.ds(t * LANES, LANES)
        top = edges[0, :, 0, lanes]
        bottom = edges[1, :, ROWS - 1, lanes]
        rows = pl.ds(t * lag_count, lag_count)
        near_ref[rows] = jnp.where(low, bottom, top)
        next_ref[rows] = jnp.where(low, top, bottom)


def pack_kernel(pieces, edge_rows, sends, *refs):
    number = 1 + max(f for _, group in sends for f in group)
    mine, near_ref, out = refs[:number], refs[number], refs[number + 1 :]
    for (at, group), out_ref in zip(sends, out):
        for place, f in enumerate(group):
            rows = pl.ds(at * LANES, LANES)
            out_ref[pl.ds(2 * place * LANES, LANES)] = mine[f][rows]
            far = pl.ds(edge_rows + (f * pieces + at) * LANES, LANES)
            out_ref[pl.ds((2 * place + 1) * LANES, LANES)] = near_ref[far]


def strip_swap(part, distance):
    count = lax.axis_size("strip")
    return lax.ppermute(part, "strip", [(i, i ^ distance) for i in range(count)])


def gather_rows(image_grad, fields):
    lag_count, depth, width = image_grad.shape
    count = lax.axis_size("strip")
    snaps, all_rows, columns = fields[0].shape
    direct = columns == LANES and count >= 4 and count & (count - 1) == 0
    pieces = count // 2 if direct else 0
    number = len(fields) if direct else 0
    edge_rows = lag_count * (width // LANES)

    def buffer(rows):
        return jax.ShapeDtypeStruct((rows, LANES), jnp.float32)

    near, following, *mine = pl.pallas_call(
        functools.partial(send_kernel, pieces),
        out_shape=[buffer(edge_rows + number * pieces * LANES), buffer(edge_rows)]
        + [buffer(pieces * LANES)] * number,
        in_specs=[pl.BlockSpec(memory_space=pltpu.HBM)] * (1 + number),
        out_specs=[whole_vmem] * (2 + number),
        scratch_shapes=[pltpu.VMEM(f.shape, jnp.float32) for f in fields[:number]]
        + [pltpu.VMEM((2, lag_count, ROWS, width), jnp.float32), pltpu.SemaphoreType.DMA((2 + number,))],
        compiler_params=pltpu.CompilerParams(vmem_limit_bytes=SUM_BYTES),
        name="send_rows",
    )(*(in_hbm(a) for a in (image_grad, *fields[:number])))
    near = strip_swap(near, 1)
    following = lax.ppermute(
        following, "strip", [p for i in range(1, count, 2) for p in ((i, (i + 1) % count), ((i + 1) % count, i))]
    )
    if not direct:
        whole = []
        for field in fields:
            cut = field.reshape(snaps, count, depth, columns).transpose(1, 3, 0, 2)
            cut = lax.all_to_all(cut.reshape(count, columns, snaps * depth), "strip", 0, 0, tiled=True)
            whole.append([cut.reshape(count * columns, snaps * depth)])
        return near, following, whole, [None] * len(fields)

    everything = tuple(range(number))
    sends = [(at, everything) for at in range(1, pieces - ALONE)]
    sends += [(at, (f,)) for f in everything for at in range(pieces - ALONE, pieces)]
    out_shape = [buffer(2 * len(group) * LANES) for _, group in sends]
    packed = pl.pallas_call(
        functools.partial(pack_kernel, pieces, edge_rows, sends),
        out_shape=out_shape,
        in_specs=[whole_vmem] * (number + 1),
        out_specs=[whole_vmem] * len(out_shape),
        compiler_params=pltpu.CompilerParams(vmem_limit_bytes=SMALL_BYTES),
        name="pack_fields",
    )(*mine, near)
    sent = [strip_swap(part, 2 * at) for (at, _), part in zip(sends, packed)]
    whole, where_at = [], []
    for f in range(number):
        came = [(at, group.index(f), part) for (at, group), part in zip(sends, sent) if f in group]
        whole.append([mine[f], near] + [part for _, _, part in came])
        where_at.append([(0, 0, 0), (1, edge_rows + f * pieces * LANES, 1)])
        for index, (at, place, _) in enumerate(came):
            for side in range(2):
                where_at[f].append((2 + index, (2 * place + side) * LANES, 2 * at + side))
    return near, following, whole, where_at


def exchange(parts, distance):
    count = lax.axis_size("lag")
    return lax.ppermute(parts, "lag", [(i, i ^ distance) for i in range(count)])


def turn_back_kernel(*refs):
    out_ref = refs[-1]
    snaps, depth, width = out_ref.shape
    for at in range(width // LANES):
        rows = pl.ds(at * LANES, LANES)
        total = refs[0][rows]
        for ref in refs[1:-1]:
            total = total + ref[rows]
        turned = total.T
        for snap in range(snaps):
            out_ref[snap, :, rows] = turned[snap * depth : (snap + 1) * depth]


def add_kernel(keep_ref, came_ref, *refs):
    rows = refs[-1].shape[0]
    refs[-1][...] = keep_ref[pl.ds(rows, rows)] + came_ref[pl.ds(rows, rows)]


def lag_send(part, *pairs):
    return lax.ppermute(part, "lag", pairs)


def sum_places(form, parts, snaps, after=()):
    if form == "direct":
        terms = [parts[0]] + [exchange(parts[d], d) for d in DIRECT_ORDER]
    elif form == "halves":
        keep, send = parts
        came = exchange(send, 1)
        rows = keep.shape[0] // 2
        passed = pl.pallas_call(
            add_kernel,
            out_shape=jax.ShapeDtypeStruct((rows, keep.shape[1]), jnp.float32),
            in_specs=[whole_vmem] * 2 + [pl.BlockSpec(memory_space=pltpu.HBM)] * len(after),
            out_specs=whole_vmem,
            compiler_params=pltpu.CompilerParams(vmem_limit_bytes=SMALL_BYTES),
            name="add_mirror",
        )(keep, came, *(in_hbm(a) for a in after))
        terms = [keep, came, exchange(passed, 3)]
    else:
        keep, second, both, mirror = parts
        rows = keep.shape[0]
        came = exchange(both, 1)
        skip = lag_send(second, (0, 2), (3, 1))
        middle = lag_send(mirror, (1, 2), (2, 1))
        passed = lag_send(second + came[:rows], (1, 3), (2, 0))
        terms = [keep, came[rows:], skip, middle, passed]
    rows, lanes = terms[-1].shape
    return pl.pallas_call(
        turn_back_kernel,
        out_shape=jax.ShapeDtypeStruct((snaps, lanes // snaps, rows), jnp.float32),
        in_specs=[whole_vmem] * len(terms),
        out_specs=whole_vmem,
        compiler_params=pltpu.CompilerParams(vmem_limit_bytes=SMALL_BYTES),
        cost_estimate=weight(BACK_COST),
        name="turn_back",
    )(*terms)


def local(image_grad, source_field, receiver_field):
    lag_count, depth, width = image_grad.shape
    snaps = source_field.shape[0]
    pad = lax.axis_size("lag") * lag_count // 2
    near, following, (receiver, source), (at_first, at_second) = gather_rows(
        image_grad, [receiver_field, source_field]
    )
    slabs = filter_slabs(image_grad, near, following, pad)
    first = sum_lags(1, FIRST_FORM, slabs, receiver, at_first, width)
    second = sum_lags(-1, SECOND_FORM, slabs, source, at_second, width, first[:1] if ORDERED else ())
    source_adjoint = sum_places(FIRST_FORM, first, snaps)
    receiver_adjoint = sum_places(SECOND_FORM, second, snaps, (source_adjoint,) if CHAIN else ())
    return source_adjoint, receiver_adjoint


def solution(mesh):
    in_specs = (P("lag", "strip", None), P(None, None, "strip"), P(None, None, "strip"))
    out_specs = (P(None, "strip", "lag"), P(None, "strip", "lag"))
    return jax.shard_map(local, mesh=mesh, in_specs=in_specs, out_specs=out_specs, check_vma=False)
```

```python
import functools

import jax
import jax.numpy as jnp
from jax import lax
from jax.experimental import pallas as pl
from jax.experimental.pallas import tpu as pltpu
from jax.sharding import PartitionSpec as P

LANES = 128
ROWS = 8
CLASSES = 4
PAIRS = 4
CHUNK = 512
ALONE = 1
FIRST_FORM = "halves"
SECOND_FORM = "direct"
ORDERED = True
GRAD_IN_HBM = True
FILTER_COST = 3 * 10**9
FIRST_COST = 0
SECOND_COST = 10**9
BACK_COST = 5 * 10**10
CHAIN = True
DIRECT_ORDER = (2, 3, 1)
FILTER_BYTES = 32 * 1024 * 1024
SUM_BYTES = 8 * 1024 * 1024
SMALL_BYTES = 4 * 1024 * 1024

def weight(size):
    return pl.CostEstimate(flops=size, bytes_accessed=min(size, 10**7), transcendentals=0)


def in_hbm(array):
    return pltpu.with_memory_space_constraint(array, pltpu.HBM)


whole_vmem = pl.BlockSpec(memory_space=pltpu.VMEM)


def filter_kernel(pad, grad_hbm, near_ref, next_ref, out_ref, edge_parts, held, sems, *turned):
    lag_count, depth, width = grad_hbm.shape
    half = lag_count // 2
    tiles = width // LANES
    steps = half // PAIRS

    def fetch(step, side):
        lags = pl.ds(step * PAIRS + side * half, PAIRS)
        return pltpu.make_async_copy(grad_hbm.at[lags], held.at[lags], sems.at[2 * step + side])

    for step in range(steps):
        for side in range(2):
            fetch(step, side).start()

    centers = turned
    strip = lax.axis_index("strip")
    core = lax.rem(strip, 2)
    inside = (strip != 0) & (strip != lax.axis_size("strip") - 1)
    blank = jnp.zeros((LANES - 2 * lag_count, LANES), jnp.float32)

    def split(value):
        high = value.astype(jnp.bfloat16)
        return high, (value - high.astype(jnp.float32)).astype(jnp.bfloat16)

    for t in range(tiles):
        rows = pl.ds(t * lag_count, lag_count)
        near, following = near_ref[rows], jnp.where(inside, next_ref[rows], 0.0)
        above = jnp.where(core == 0, following, near)
        below = jnp.where(core == 0, near, following)
        parts = split(jnp.concatenate([above, below, blank], 0).T)
        for part in range(2):
            edge_parts[part, pl.ds(t * LANES, LANES)] = parts[part]
    out_ref[:, pl.ds(0, pad)] = jnp.zeros((half, pad, LANES), jnp.float32)
    out_ref[:, pl.ds(pad + width, pad)] = jnp.zeros((half, pad, LANES), jnp.float32)
    for center_t in centers:
        center_t[pl.ds(0, ROWS)] = jnp.zeros((ROWS, LANES), jnp.float32)
        center_t[pl.ds(ROWS + width, ROWS)] = jnp.zeros((ROWS, LANES), jnp.float32)

    def body(step, carry):
        fetch(step, 0).wait()
        fetch(step, 1).wait()
        low_ref, high_ref = held.at[pl.ds(step * PAIRS, PAIRS)], held.at[pl.ds(step * PAIRS + half, PAIRS)]
        source = lax.broadcasted_iota(jnp.int32, (LANES, LANES), 0)
        target = lax.broadcasted_iota(jnp.int32, (LANES, LANES), 1)
        beside = (jnp.abs(source - target) == 1) & ((source < depth) == (target < depth))
        band = jnp.where(source == target, 2.0, jnp.where(beside, -0.25, 0.0))
        upper = jnp.where(target == 0, 0, jnp.where(target == depth, half, 2 * LANES))
        lower = jnp.where(target == depth - 1, 0, jnp.where(target == 2 * depth - 1, half, 2 * LANES))
        matrices = []
        for within in range(PAIRS):
            lag = step * PAIRS + within
            chosen = (source == upper + lag) | (source == lower + lag + lag_count)
            choice = jnp.where(chosen, -0.25, 0.0)
            matrices.append(jnp.concatenate([band, choice], 0).astype(jnp.bfloat16))

        def turn(within, t):
            rows = pl.ds(t * LANES, LANES)
            center = jnp.concatenate([low_ref[within, :, rows], high_ref[within, :, rows]], 0).T
            centers[within][pl.ds(ROWS + t * LANES, LANES)] = center

        def join(within, at):
            rows = pl.ds(at * chunk, chunk)
            west = centers[within][pl.ds(ROWS - 1 + at * chunk, chunk)]
            east = centers[within][pl.ds(ROWS + 1 + at * chunk, chunk)]
            parts = split(centers[within][pl.ds(ROWS + at * chunk, chunk)])
            products = [
                jnp.dot(
                    jnp.concatenate([parts[part], edge_parts[part, rows]], 1),
                    matrices[within],
                    preferred_element_type=jnp.float32,
                )
                for part in range(2)
            ]
            value = (products[0] + products[1]) - 0.25 * (west + east)
            out_ref[step * PAIRS + within, pl.ds(pad + at * chunk, chunk)] = value

        chunk = min(CHUNK, width)
        for within in range(PAIRS + 1):
            for t in range(tiles):
                if within < PAIRS:
                    turn(within, t)
                if within and (t + 1) * LANES % chunk == 0:
                    join(within - 1, ((t + 1) * LANES // chunk) - 1)
        return carry

    lax.fori_loop(0, steps, body, 0)


def filter_slabs(image_grad, from_near, from_next, pad):
    lag_count, depth, width = image_grad.shape
    return pl.pallas_call(
        functools.partial(filter_kernel, pad),
        out_shape=jax.ShapeDtypeStruct((lag_count // 2, width + 2 * pad, 2 * depth), jnp.float32),
        in_specs=[pl.BlockSpec(memory_space=pltpu.HBM if GRAD_IN_HBM else pl.ANY), whole_vmem, whole_vmem],
        out_specs=whole_vmem,
        scratch_shapes=[pltpu.VMEM((2, width, LANES), jnp.bfloat16)]
        + [pltpu.VMEM(image_grad.shape, jnp.float32), pltpu.SemaphoreType.DMA((lag_count // PAIRS,))]
        + [pltpu.VMEM((width + 2 * ROWS, LANES), jnp.float32)] * PAIRS,
        compiler_params=pltpu.CompilerParams(vmem_limit_bytes=FILTER_BYTES),
        cost_estimate=weight(FILTER_COST),
        name="filter_slabs",
    )(in_hbm(image_grad) if GRAD_IN_HBM else image_grad, from_near, from_next)


def sum_kernel(sign, places, where_at, blocks, slab_ref, *refs):
    number = len(blocks)
    pieces, outs = refs[: -3 - number], refs[-3 - number : -3]
    field_ref, paired, acc = refs[-3:]
    half, slab_rows, _ = slab_ref.shape
    width = field_ref.shape[0]
    if where_at is None:
        field_ref[...] = pieces[0][...]
    else:
        strip = lax.axis_index("strip")
        for index, row, distance in where_at:
            rows = pl.multiple_of((strip ^ distance) * LANES, LANES)
            field_ref[pl.ds(rows, LANES)] = pieces[index][pl.ds(row, LANES)]
    pad = (slab_rows - width) // 2
    lag_count = 2 * half
    margin = 2 * pad + 2 * half
    place = lax.axis_index("lag")
    first = place * lag_count - pad
    spread = width + half
    block_rows = ROWS * max(m for m in range(1, 14) if spread // ROWS % m == 0)
    low_at = 0 if sign > 0 else half
    high_at = half - low_at

    for snap in range(2):
        blank = jnp.zeros((margin + half, LANES), jnp.float32)
        paired[snap, pl.ds(0, margin)] = blank[:margin]
        paired[snap, pl.ds(margin + width, margin)] = blank[:margin]
    low = lax.broadcasted_iota(jnp.int32, (LANES, LANES), 1) < LANES // 2
    edge = jnp.zeros((half, LANES), jnp.float32)
    field = field_ref[...]
    lower = lax.broadcasted_iota(jnp.int32, (spread, LANES), 1) < LANES // 2
    if sign > 0:
        here = jnp.concatenate([edge, field], 0)
        there = jnp.concatenate([field, edge], 0)
        start = margin - half
    else:
        here = jnp.concatenate([field, edge], 0)
        there = jnp.concatenate([edge, field], 0)
        start = margin
    paired[0, pl.ds(start, spread)] = jnp.where(lower, here, pltpu.roll(there, LANES // 2, 1))
    paired[1, pl.ds(start, spread)] = jnp.where(lower, pltpu.roll(here, LANES // 2, 1), there)

    tall = block_rows // ROWS
    per_class = half // CLASSES

    def block(at, carry):
        y = at * block_rows - low_at
        slab_at = pl.multiple_of(pad + y + sign * first, ROWS)
        field_at = pl.multiple_of(margin + y + sign * 2 * first, ROWS)
        totals = [[None] * tall for _ in range(2)]
        for cls in range(CLASSES):
            held = {}
            for step in range(per_class):
                lag = step * CLASSES + cls
                for up in range(tall):
                    slab = slab_ref[lag, pl.ds(slab_at + sign * lag + up * ROWS, ROWS)]
                    for snap in range(2):
                        row = sign * 2 * lag + up * ROWS
                        if (snap, row) not in held:
                            held[snap, row] = paired[snap, pl.ds(field_at + row, ROWS)]
                        term = slab * held[snap, row]
                        total = totals[snap][up]
                        totals[snap][up] = term if total is None else total + term
        for snap in range(2):
            for up in range(tall):
                rows = pl.multiple_of(at * block_rows + up * ROWS, ROWS)
                acc[snap, pl.ds(rows, ROWS)] = totals[snap][up]
        return carry

    lax.fori_loop(0, spread // block_rows, block, 0)

    part = width // places

    def finish(target, slot, source):
        for piece in range(part // LANES):
            x = pl.multiple_of(source * part + piece * LANES, LANES)
            at_low = pl.ds(x + low_at, LANES)
            at_high = pl.ds(x + high_at, LANES)
            straight = jnp.where(low, acc[0, at_low], acc[1, at_high])
            crossed = jnp.where(low, acc[1, at_low], acc[0, at_high])
            rows = pl.ds(slot * part + piece * LANES, LANES)
            target[rows] = straight + pltpu.roll(crossed, LANES // 2, 1)

    for target, distances in zip(outs, blocks):
        for slot, distance in enumerate(distances):
            finish(target, slot, place ^ distance)


BLOCKS = {
    "direct": ((0,), (1,), (2,), (3,)),
    "halves": ((0, 3), (1, 2)),
    "forward": ((0,), (2,), (3, 1), (3,)),
}


def sum_lags(sign, form, slabs, pieces, where_at, width, after=()):
    half, slab_rows, _ = slabs.shape
    pad = (slab_rows - width) // 2
    margin = 2 * pad + 2 * half
    places = lax.axis_size("lag")
    part = width // places
    out_shape = [jax.ShapeDtypeStruct((len(held) * part, LANES), jnp.float32) for held in BLOCKS[form]]
    return pl.pallas_call(
        functools.partial(sum_kernel, sign, places, where_at, BLOCKS[form]),
        out_shape=out_shape,
        in_specs=[whole_vmem] * (1 + len(pieces) + len(after)),
        out_specs=[whole_vmem] * len(out_shape),
        scratch_shapes=[
            pltpu.VMEM((width, LANES), jnp.float32),
            pltpu.VMEM((2, width + 2 * margin, LANES), jnp.float32),
            pltpu.VMEM((2, width + half, LANES), jnp.float32),
        ],
        compiler_params=pltpu.CompilerParams(vmem_limit_bytes=SUM_BYTES),
        cost_estimate=weight(FIRST_COST if sign > 0 else SECOND_COST),
        name="sum_lags",
    )(slabs, *pieces, *after)


def send_kernel(pieces, grad_hbm, *refs):
    lag_count, depth, width = grad_hbm.shape
    tiles = width // LANES
    number = (len(refs) - 4) // 3
    fields, near_ref, next_ref = refs[:number], refs[number], refs[number + 1]
    mine = refs[number + 2 : 2 * number + 2]
    held, edges, sems = refs[2 * number + 2 : 3 * number + 2], refs[-2], refs[-1]
    strip = lax.axis_index("strip")
    core = lax.rem(strip, 2)
    copies = []
    for side in range(2):
        rows = pl.ds(side * (depth - ROWS), ROWS)
        copies.append(pltpu.make_async_copy(grad_hbm.at[:, rows], edges.at[side], sems.at[side]))
    for f in range(number):
        copies.append(pltpu.make_async_copy(fields[f], held[f], sems.at[2 + f]))
    for copy in copies[2:] + copies[:2]:
        copy.start()

    for f in range(number):
        copies[2 + f].wait()
        snaps = held[f].shape[0]
        for at in range(pieces):
            for side in range(2):
                first = pl.multiple_of((strip ^ (2 * at + side)) * depth, depth)
                rows = [held[f][s, pl.ds(first, depth)] for s in range(snaps)]
                piece = jnp.concatenate(rows, 0).T
                if side:
                    start = lag_count * tiles + (f * pieces + at) * LANES
                    near_ref[pl.ds(start, LANES)] = piece
                else:
                    mine[f][pl.ds(at * LANES, LANES)] = piece

    copies[0].wait()
    copies[1].wait()
    low = core == 0
    for t in range(tiles):
        lanes = pl.ds(t * LANES, LANES)
        top = edges[0, :, 0, lanes]
        bottom = edges[1, :, ROWS - 1, lanes]
        rows = pl.ds(t * lag_count, lag_count)
        near_ref[rows] = jnp.where(low, bottom, top)
        next_ref[rows] = jnp.where(low, top, bottom)


def pack_kernel(pieces, edge_rows, sends, *refs):
    number = 1 + max(f for _, group in sends for f in group)
    mine, near_ref, out = refs[:number], refs[number], refs[number + 1 :]
    for (at, group), out_ref in zip(sends, out):
        for place, f in enumerate(group):
            rows = pl.ds(at * LANES, LANES)
            out_ref[pl.ds(2 * place * LANES, LANES)] = mine[f][rows]
            far = pl.ds(edge_rows + (f * pieces + at) * LANES, LANES)
            out_ref[pl.ds((2 * place + 1) * LANES, LANES)] = near_ref[far]


def strip_swap(part, distance):
    count = lax.axis_size("strip")
    return lax.ppermute(part, "strip", [(i, i ^ distance) for i in range(count)])


def gather_rows(image_grad, fields):
    lag_count, depth, width = image_grad.shape
    count = lax.axis_size("strip")
    snaps, all_rows, columns = fields[0].shape
    direct = columns == LANES and count >= 4 and count & (count - 1) == 0
    pieces = count // 2 if direct else 0
    number = len(fields) if direct else 0
    edge_rows = lag_count * (width // LANES)

    def buffer(rows):
        return jax.ShapeDtypeStruct((rows, LANES), jnp.float32)

    near, following, *mine = pl.pallas_call(
        functools.partial(send_kernel, pieces),
        out_shape=[buffer(edge_rows + number * pieces * LANES), buffer(edge_rows)]
        + [buffer(pieces * LANES)] * number,
        in_specs=[pl.BlockSpec(memory_space=pltpu.HBM)] * (1 + number),
        out_specs=[whole_vmem] * (2 + number),
        scratch_shapes=[pltpu.VMEM(f.shape, jnp.float32) for f in fields[:number]]
        + [pltpu.VMEM((2, lag_count, ROWS, width), jnp.float32), pltpu.SemaphoreType.DMA((2 + number,))],
        compiler_params=pltpu.CompilerParams(vmem_limit_bytes=SUM_BYTES),
        name="send_rows",
    )(*(in_hbm(a) for a in (image_grad, *fields[:number])))
    near = strip_swap(near, 1)
    following = lax.ppermute(
        following, "strip", [p for i in range(1, count, 2) for p in ((i, (i + 1) % count), ((i + 1) % count, i))]
    )
    if not direct:
        whole = []
        for field in fields:
            cut = field.reshape(snaps, count, depth, columns).transpose(1, 3, 0, 2)
            cut = lax.all_to_all(cut.reshape(count, columns, snaps * depth), "strip", 0, 0, tiled=True)
            whole.append([cut.reshape(count * columns, snaps * depth)])
        return near, following, whole, [None] * len(fields)

    everything = tuple(range(number))
    sends = [(at, everything) for at in range(1, pieces - ALONE)]
    sends += [(at, (f,)) for f in everything for at in range(pieces - ALONE, pieces)]
    out_shape = [buffer(2 * len(group) * LANES) for _, group in sends]
    packed = pl.pallas_call(
        functools.partial(pack_kernel, pieces, edge_rows, sends),
        out_shape=out_shape,
        in_specs=[whole_vmem] * (number + 1),
        out_specs=[whole_vmem] * len(out_shape),
        compiler_params=pltpu.CompilerParams(vmem_limit_bytes=SMALL_BYTES),
        name="pack_fields",
    )(*mine, near)
    sent = [strip_swap(part, 2 * at) for (at, _), part in zip(sends, packed)]
    whole, where_at = [], []
    for f in range(number):
        came = [(at, group.index(f), part) for (at, group), part in zip(sends, sent) if f in group]
        whole.append([mine[f], near] + [part for _, _, part in came])
        where_at.append([(0, 0, 0), (1, edge_rows + f * pieces * LANES, 1)])
        for index, (at, place, _) in enumerate(came):
            for side in range(2):
                where_at[f].append((2 + index, (2 * place + side) * LANES, 2 * at + side))
    return near, following, whole, where_at


def exchange(parts, distance):
    count = lax.axis_size("lag")
    return lax.ppermute(parts, "lag", [(i, i ^ distance) for i in range(count)])


def turn_back_kernel(*refs):
    out_ref = refs[-1]
    snaps, depth, width = out_ref.shape
    for at in range(width // LANES):
        rows = pl.ds(at * LANES, LANES)
        total = refs[0][rows]
        for ref in refs[1:-1]:
            total = total + ref[rows]
        turned = total.T
        for snap in range(snaps):
            out_ref[snap, :, rows] = turned[snap * depth : (snap + 1) * depth]


def add_kernel(keep_ref, came_ref, *refs):
    rows = refs[-1].shape[0]
    refs[-1][...] = keep_ref[pl.ds(rows, rows)] + came_ref[pl.ds(rows, rows)]


def lag_send(part, *pairs):
    return lax.ppermute(part, "lag", pairs)


def sum_places(form, parts, snaps, after=()):
    if form == "direct":
        terms = [parts[0]] + [exchange(parts[d], d) for d in DIRECT_ORDER]
    elif form == "halves":
        keep, send = parts
        came = exchange(send, 1)
        rows = keep.shape[0] // 2
        passed = pl.pallas_call(
            add_kernel,
            out_shape=jax.ShapeDtypeStruct((rows, keep.shape[1]), jnp.float32),
            in_specs=[whole_vmem] * 2 + [pl.BlockSpec(memory_space=pltpu.HBM)] * len(after),
            out_specs=whole_vmem,
            compiler_params=pltpu.CompilerParams(vmem_limit_bytes=SMALL_BYTES),
            name="add_mirror",
        )(keep, came, *(in_hbm(a) for a in after))
        terms = [keep, came, exchange(passed, 3)]
    else:
        keep, second, both, mirror = parts
        rows = keep.shape[0]
        came = exchange(both, 1)
        skip = lag_send(second, (0, 2), (3, 1))
        middle = lag_send(mirror, (1, 2), (2, 1))
        passed = lag_send(second + came[:rows], (1, 3), (2, 0))
        terms = [keep, came[rows:], skip, middle, passed]
    rows, lanes = terms[-1].shape
    return pl.pallas_call(
        turn_back_kernel,
        out_shape=jax.ShapeDtypeStruct((snaps, lanes // snaps, rows), jnp.float32),
        in_specs=[whole_vmem] * len(terms),
        out_specs=whole_vmem,
        compiler_params=pltpu.CompilerParams(vmem_limit_bytes=SMALL_BYTES),
        cost_estimate=weight(BACK_COST),
        name="turn_back",
    )(*terms)


def local(image_grad, source_field, receiver_field):
    lag_count, depth, width = image_grad.shape
    snaps = source_field.shape[0]
    pad = lax.axis_size("lag") * lag_count // 2
    near, following, (receiver, source), (at_first, at_second) = gather_rows(
        image_grad, [receiver_field, source_field]
    )
    slabs = filter_slabs(image_grad, near, following, pad)
    first = sum_lags(1, FIRST_FORM, slabs, receiver, at_first, width)
    second = sum_lags(-1, SECOND_FORM, slabs, source, at_second, width, first[:1] if ORDERED else ())
    source_adjoint = sum_places(FIRST_FORM, first, snaps)
    receiver_adjoint = sum_places(SECOND_FORM, second, snaps, (source_adjoint,) if CHAIN else ())
    return source_adjoint, receiver_adjoint


def solution(mesh):
    in_specs = (P("lag", "strip", None), P(None, None, "strip"), P(None, None, "strip"))
    out_specs = (P(None, "strip", "lag"), P(None, "strip", "lag"))
    return jax.shard_map(local, mesh=mesh, in_specs=in_specs, out_specs=out_specs, check_vma=False)
```
